512 devices in a mesh: req: 32 (over x, y), seq: 16 (over z, core).
Axes of the slice: x: 4, y: 8, z: 8, core: 2. Of those that a mesh axis runs over, the one named last changes fastest.
Arguments:
- q_slots: bfloat16 [65536, 4096], P(('req', 'seq')), parts along dimension 0, may hold values from -240 to 240
- k_cache: bfloat16 [65536, 4096], P(('req', 'seq')), parts along dimension 0, may hold values from -6 to 6
- v_cache: bfloat16 [65536, 4096], P(('req', 'seq')), parts along dimension 0, may hold values from -6 to 6
- tiles: int32 [512, 2], P(('req', 'seq')), parts along dimension 0, may hold values from -1 to 1, as said below
Outputs:
- refreshed: bfloat16 [65536, 4096], P(('req', 'seq')), parts along dimension 0
The draws below stay inside these ranges and needn't reach their ends.
There are 32 independent parts, one for each index of `req`. The reference program is written for one: setup_inputs(seed, part) draws one part's arguments, and reference() takes and returns one part's arrays. A program takes and returns all parts, laid end to end along the dimension named above; each array names one. Nothing has to cross between parts.
Inputs may be any that keep to these rules, and one draw needn't show every extreme that they name: `tiles`: in each row the live entries come first, distinct and ascending, and the rest are -1. Exactly 12 entries of a request are live, and some index of seq has all 2 slots live.
All inputs are finite; a program needn't handle non-finite values.
Results may differ from the reference program's by a relative error of at most 0.02.
The reference program's roundings to bfloat16 on the way (of `rotated` and `probs`) count: a program that leaves them out, or rounds other values in their place, can miss the bound.
Values may be sent and summed in bfloat16 or wider, within the bound.
A program may use at most 64 MiB of HBM per device.

```python
import jax
import jax.numpy as jnp
from jax import lax

H = 32
DH = 128
HD = 4096
TILE = 64
TPD = 2
L = 2048
REFRESHED = 12
N_SEQ = 16


def draw_q_slots(key, part):
    key = jax.random.fold_in(key, 11)
    first_key = jax.random.fold_in(key, 0)
    row_count = N_SEQ * TPD * TILE
    shape = (row_count, H * DH)
    base = jnp.clip(jax.random.normal(first_key, shape, jnp.float32), -6.0, 6.0)
    return base.astype(jnp.bfloat16)


def draw_tiles(key, part):
    key = jax.random.fold_in(key, 5)
    first_key, second_key = jax.random.split(key)
    tile_count = N_SEQ * TPD
    full_shard = jax.random.randint(first_key, (), 0, N_SEQ)
    owner = jnp.arange(tile_count, dtype=jnp.int32) // TPD
    forced = owner == full_shard
    shuffled = jax.random.permutation(second_key, tile_count).astype(jnp.int32)
    priority = jnp.where(forced, -1, shuffled)
    ordering = jnp.argsort(priority, stable=True)
    chosen = jnp.zeros((tile_count,), jnp.int32).at[ordering[:REFRESHED]].set(1)
    grid_live = chosen.reshape(N_SEQ, TPD) > 0
    local = jnp.arange(TPD, dtype=jnp.int32)[None, :]
    ranked = jnp.sort(jnp.where(grid_live, local, TPD + local), axis=1)
    return jnp.where(ranked < TPD, ranked, -1).astype(jnp.int32)


def block_levels(rng, shape, cuts, least, high):
    level = 1.0
    for dim, shards_of in cuts:
        heights = jax.random.uniform(jax.random.fold_in(jax.random.fold_in(rng, 6), dim), (shards_of,), jnp.float32, least / len(cuts), high / len(cuts))
        level = level * jnp.repeat(jnp.exp(heights), shape[dim] // shards_of).reshape((-1,) + (1,) * (len(shape) - 1 - dim))
    return level


def scatter_about(rng, shape, deviation, limit, shards=(), kind=jnp.bfloat16):
    entries = jax.random.normal(rng, shape, jnp.float32) * deviation
    if len(shards) > 0:
        entries = block_levels(rng, shape, shards, -0.22, 0.18) * entries
    return jnp.clip(entries, min=-limit, max=limit).astype(kind)


def setup_inputs(seed: int = 0, part: int = 0) -> dict:
    seeds = jax.random.split(jax.random.key(seed), 5)
    own_keys = jax.random.split(jax.random.fold_in(seeds[4], part), 5)
    return {
        "q_slots": draw_q_slots(jax.random.fold_in(jax.random.fold_in(seeds[4], part), 71), part),
        "k_cache": scatter_about(own_keys[1], (L, HD), 1.0, 6.0, ((0, 16),)),
        "v_cache": scatter_about(own_keys[2], (L, HD), 1.0, 6.0, ((0, 16),)),
        "tiles": draw_tiles(jax.random.fold_in(jax.random.fold_in(seeds[4], part), 71), part),
    }


def rotate(values, position):
    half_dim = DH // 2
    inverse = 10000.0 ** (-jnp.arange(half_dim, dtype=jnp.float32) / half_dim)
    angles = position[..., None, None] * inverse
    cosine = jnp.cos(angles)
    sine = jnp.sin(angles)
    first = values[..., :half_dim]
    second = values[..., half_dim:]
    return jnp.concatenate([first * cosine - second * sine, second * cosine + first * sine], axis=-1)


def reference(q_slots, k_cache, v_cache, tiles):
    live = tiles >= 0
    shard_ids = jnp.arange(N_SEQ, dtype=jnp.int32)[:, None]
    global_tile = shard_ids * TPD + jnp.maximum(tiles, 0)
    position = (global_tile[:, :, None] * TILE + jnp.arange(TILE, dtype=jnp.int32)).reshape(-1).astype(jnp.float32)
    slot_rows = q_slots.shape[0]
    queries = q_slots.astype(jnp.float32).reshape(slot_rows, H, DH)
    rotated = rotate(queries, position).astype(jnp.bfloat16)
    key_rows = k_cache.reshape(L, H, DH)
    value_rows = v_cache.reshape(L, H, DH)

    def one_head(index):
        q_head = lax.dynamic_index_in_dim(rotated, index, 1, keepdims=False)
        k_head = lax.dynamic_index_in_dim(key_rows, index, 1, keepdims=False)
        v_head = lax.dynamic_index_in_dim(value_rows, index, 1, keepdims=False)
        scores = jnp.dot(q_head, k_head.T, preferred_element_type=jnp.float32) * (DH ** -0.5)
        largest = jnp.max(scores, axis=-1, keepdims=True)
        expsum = jnp.exp(scores - largest)
        probs = (expsum / jnp.sum(expsum, axis=-1, keepdims=True)).astype(jnp.bfloat16)
        return jnp.dot(probs, v_head, preferred_element_type=jnp.float32).astype(jnp.bfloat16)

    heads_out = lax.map(one_head, jnp.arange(H, dtype=jnp.int32))
    attended = jnp.transpose(heads_out, (1, 0, 2)).reshape(slot_rows, H * DH)
    row_live = jnp.repeat(live.reshape(-1), TILE)
    return jnp.where(row_live[:, None], attended, jnp.zeros((), jnp.bfloat16))
```

```python
import functools
import math

import jax
import jax.numpy as jnp
import numpy as np
from jax import lax
from jax.experimental import pallas as pl
from jax.experimental.pallas import tpu as pltpu
from jax.sharding import PartitionSpec as P

MESH = pl.DeviceIdType.MESH
DH = 128


def kernel(n, tiles_ref, inv_ref, q_ref, k_ref, v_ref, o_ref,
           q_in, q_rot, q_all, k_all, v_all, probs, norm, o_send,
           local_sem, k_send, k_recv, v_send, v_recv, q_send, q_recv, o_ssem, o_rsem):
    me = lax.axis_index("seq")
    rows, width = q_in.shape
    local = width // n
    heads = local // DH
    tile_rows = rows // 2
    keys = n * rows

    def cols(index):
        return pl.ds(pl.multiple_of(index * local, local), local)

    def span(index):
        return pl.ds(pl.multiple_of(index * rows, rows), rows)

    def peer(offset):
        return lax.rem(me + offset, n)

    barrier = pltpu.get_barrier_semaphore()
    for offset in range(1, n):
        pl.semaphore_signal(barrier, inc=1, device_id={"seq": peer(offset)}, device_id_type=MESH)
    load_q = pltpu.make_async_copy(q_ref, q_in, local_sem.at[0])
    load_q.start()
    own_k = pltpu.make_async_copy(k_ref.at[:, cols(me)], k_all.at[span(me), :], local_sem.at[1])
    own_k.start()
    own_v = pltpu.make_async_copy(v_ref.at[:, cols(me)], v_all.at[span(me), :], local_sem.at[2])
    own_v.start()
    pl.semaphore_wait(barrier, n - 1)

    def send(source, target, send_sem, recv_sem, offset):
        to = peer(offset)
        return pltpu.make_async_remote_copy(
            src_ref=source.at[:, cols(to)],
            dst_ref=target.at[span(me), :],
            send_sem=send_sem.at[offset],
            recv_sem=recv_sem.at[offset],
            device_id={"seq": to},
            device_id_type=MESH,
        )

    send_k = functools.partial(send, k_ref, k_all, k_send, k_recv)
    send_v = functools.partial(send, v_ref, v_all, v_send, v_recv)
    send_q = functools.partial(send, q_rot, q_all, q_send, q_recv)

    def send_o(offset):
        to = peer(offset)
        return pltpu.make_async_remote_copy(
            src_ref=o_send.at[span(to), :],
            dst_ref=o_ref.at[:, cols(me)],
            send_sem=o_ssem.at[offset],
            recv_sem=o_rsem.at[offset],
            device_id={"seq": to},
            device_id_type=MESH,
        )

    order = []
    for step in range(1, n // 2 + 1):
        order += [step] if step == n // 2 else [step, n - step]

    for offset in order:
        send_k(offset).start()

    row = lax.broadcasted_iota(jnp.int32, (rows, DH), 0)
    lane = lax.broadcasted_iota(jnp.int32, (rows, DH), 1)
    first = jnp.maximum(tiles_ref[0, 0], 0) * tile_rows
    second = (jnp.maximum(tiles_ref[0, 1], 0) - 1) * tile_rows
    position = (me * rows + row + jnp.where(row < tile_rows, first, second)).astype(jnp.float32)
    angles = position * inv_ref[0:1, :]
    cosine = jnp.cos(angles)
    sine = jnp.where(lane < DH // 2, -jnp.sin(angles), jnp.sin(angles))
    load_q.wait()

    def rotate(head, carry):
        at = pl.ds(pl.multiple_of(head * DH, DH), DH)
        value = q_in[:, at].astype(jnp.float32)
        swapped = pltpu.roll(value, DH // 2, axis=1)
        q_rot[:, at] = (value * cosine + swapped * sine).astype(jnp.bfloat16)
        return carry

    lax.fori_loop(0, width // DH, rotate, 0)
    for offset in order:
        send_q(offset).start()
    for offset in order:
        send_v(offset).start()
    q_all[span(me), :] = q_rot[:, cols(me)]

    own_k.wait()
    for offset in order:
        send_k(offset).wait_recv()

    factor = math.log2(math.e) / math.sqrt(DH)

    def score(offset, carry):
        source = peer(n - offset)

        @pl.when(offset > 0)
        def _():
            send_q(offset).wait_recv()

        for head in range(heads):
            at = pl.ds(head * DH, DH)
            logits = lax.dot_general(
                q_all[span(source), at], k_all[:, at],
                (((1,), (1,)), ((), ())), preferred_element_type=jnp.float32,
            )
            largest = jnp.max(logits, axis=1, keepdims=True)
            weight = jnp.exp2((logits - largest) * factor)
            norm[span(source), at] = jnp.broadcast_to(
                1.0 / jnp.sum(weight, axis=1, keepdims=True), (rows, DH)
            )
            probs[head, span(source), :] = weight.astype(jnp.bfloat16)
        return carry

    lax.fori_loop(0, n, score, 0)

    own_v.wait()
    for offset in order:
        send_v(offset).wait_recv()

    def combine(step, carry):
        offset = lax.rem(step + 1, n)
        source = peer(offset)
        for head in range(heads):
            at = pl.ds(head * DH, DH)
            total = jnp.dot(
                probs[head, span(source), :], v_all[:, at], preferred_element_type=jnp.float32
            )
            o_send[span(source), at] = (total * norm[span(source), at]).astype(jnp.bfloat16)

        @pl.when(offset > 0)
        def _():
            send_o(offset).start()

        return carry

    lax.fori_loop(0, n, combine, 0)
    o_ref[:, cols(me)] = o_send[span(me), :]
    for offset in order:
        send_k(offset).wait_send()
        send_q(offset).wait_send()
        send_v(offset).wait_send()
    for offset in order:
        send_o(offset).wait()


def on_device(n, q_slots, k_cache, v_cache, tiles):
    rows, width = q_slots.shape
    local = width // n
    half = DH // 2
    inverse = 10000.0 ** (-np.arange(half) / half)
    inverse = jnp.asarray(np.broadcast_to(np.tile(inverse, 2)[None, :], (8, DH)), jnp.float32)
    dma = pltpu.SemaphoreType.DMA
    attended = pl.pallas_call(
        functools.partial(kernel, n),
        out_shape=jax.ShapeDtypeStruct((rows, width), jnp.bfloat16),
        in_specs=[
            pl.BlockSpec(memory_space=pltpu.SMEM),
            pl.BlockSpec(memory_space=pltpu.VMEM),
            pl.BlockSpec(memory_space=pl.ANY),
            pl.BlockSpec(memory_space=pl.ANY),
            pl.BlockSpec(memory_space=pl.ANY),
        ],
        out_specs=pl.BlockSpec(memory_space=pltpu.VMEM),
        scratch_shapes=[
            pltpu.VMEM((rows, width), jnp.bfloat16),
            pltpu.VMEM((rows, width), jnp.bfloat16),
            pltpu.VMEM((n * rows, local), jnp.bfloat16),
            pltpu.VMEM((n * rows, local), jnp.bfloat16),
            pltpu.VMEM((n * rows, local), jnp.bfloat16),
            pltpu.VMEM((local // DH, n * rows, n * rows), jnp.bfloat16),
            pltpu.VMEM((n * rows, local), jnp.float32),
            pltpu.VMEM((n * rows, local), jnp.bfloat16),
            dma((3,)),
        ] + [dma((n,))] * 8,
        name="refresh_attention",
        compiler_params=pltpu.CompilerParams(
            collective_id=0, has_side_effects=True, vmem_limit_bytes=56 * 2**20
        ),
    )(tiles, inverse, q_slots, k_cache, v_cache)
    live = jnp.repeat(tiles[0] >= 0, rows // tiles.shape[1])
    return jnp.where(live[:, None], attended, jnp.zeros((), jnp.bfloat16))


def solution(mesh):
    spec = P(("req", "seq"), None)
    return jax.shard_map(
        functools.partial(on_device, mesh.shape["seq"]),
        mesh=mesh, in_specs=(spec,) * 4, out_specs=spec, check_vma=False,
    )
```

```python
import functools
import math

import jax
import jax.numpy as jnp
import numpy as np
from jax import lax
from jax.experimental import pallas as pl
from jax.experimental.layout import Layout, with_layout_constraint
from jax.experimental.pallas import tpu as pltpu
from jax.sharding import PartitionSpec as P

MESH = pl.DeviceIdType.MESH
DH = 128
HALF = DH // 2
TILE = 64
SLOTS = 2
LIVE = 12
HEADS = 2
LOCAL = HEADS * DH
N = 16
CHIPS = N // 2
ROWS = SLOTS * TILE
ROOM = {1: 8, 2: 6, 3: 5, 4: 3, 5: 1, 6: 0, 7: 0}
HOPS = 5
PACE = (12, 4, 4, 4, 4, 4)


def kernel(tiles_ref, inv_ref, q_ref, k_ref, v_ref, o_ref, flag_ref,
           q_in, q_out, q_chip, q_live, k_all, v_all, probs, norm, o_live, o_send,
           count_out, count_all, counts,
           pack_a, pack_b, land_a, land_b,
           local_sem, count_ssem, count_rsem, twin_ssem, twin_rsem,
           hop_ssem, hop_rsem, k_ssem, k_rsem, v_ssem, v_rsem, o_ssem, o_rsem):
    me = lax.axis_index("seq")
    chip = me // 2
    core = lax.rem(me, 2)

    def at(index, size):
        return pl.ds(pl.multiple_of(index * size, size), size)

    def peer(offset):
        return lax.rem(me + offset, N)

    def remote(source, target, ssem, rsem, **where):
        return pltpu.make_async_remote_copy(
            src_ref=source, dst_ref=target, send_sem=ssem, recv_sem=rsem,
            device_id=where, device_id_type=MESH,
        )

    barrier = pltpu.get_barrier_semaphore()
    for offset in range(1, N):
        pl.semaphore_signal(barrier, inc=1, device_id={"seq": peer(offset)}, device_id_type=MESH)
    load_q = pltpu.make_async_copy(q_ref, q_in, local_sem.at[0])
    load_q.start()
    own_k = pltpu.make_async_copy(k_ref.at[:, at(me, LOCAL)], k_all.at[at(me, ROWS), :], local_sem.at[1])
    own_k.start()
    own_v = pltpu.make_async_copy(v_ref.at[:, at(me, LOCAL)], v_all.at[at(me, ROWS), :], local_sem.at[2])
    own_v.start()

    first_live = (tiles_ref[0, 0] >= 0).astype(jnp.int32)
    second_live = (tiles_ref[0, 1] >= 0).astype(jnp.int32)
    count = jnp.full((8, DH), first_live + second_live, jnp.int32)
    count_out[...] = count
    count_all[me] = count
    pl.semaphore_wait(barrier, N - 1)

    def send_count(offset):
        return remote(count_out, count_all.at[me], count_ssem.at[offset], count_rsem.at[offset], seq=peer(offset))

    def send_k(offset):
        to = peer(offset)
        return remote(k_ref.at[:, at(to, LOCAL)], k_all.at[at(me, ROWS), :],
                      k_ssem.at[offset], k_rsem.at[offset], seq=to)

    def send_v(head, offset):
        to = peer(offset)
        return remote(v_ref.at[:, at(to * HEADS + head, DH)], v_all.at[at(me, ROWS), pl.ds(head * DH, DH)],
                      v_ssem.at[head, offset], v_rsem.at[head, offset], seq=to)

    def send_o(head, offset):
        to = peer(offset)
        return remote(o_send.at[offset, :, pl.ds(head * DH, DH)], o_ref.at[:, at(me * HEADS + head, DH)],
                      o_ssem.at[head, offset], o_rsem.at[head, offset], seq=to)

    order = []
    for step in range(1, N // 2 + 1):
        order += [step] if step == N // 2 else [step, N - step]
    bulk = [send_k(offset) for offset in order]
    bulk += [send_v(head, offset) for head in range(HEADS) for offset in order]
    started = 0

    def start_bulk(amount):
        nonlocal started
        for copy in bulk[started:started + amount]:
            copy.start()
        started += amount

    for offset in order:
        send_count(offset).start()
    start_bulk(PACE[0])

    row = lax.broadcasted_iota(jnp.int32, (ROWS, DH), 0)
    lane = lax.broadcasted_iota(jnp.int32, (ROWS, DH), 1)
    first = jnp.maximum(tiles_ref[0, 0], 0) * TILE
    second = (jnp.maximum(tiles_ref[0, 1], 0) - 1) * TILE
    position = (me * ROWS + row + jnp.where(row < TILE, first, second)).astype(jnp.float32)
    angles = position * inv_ref[0:1, :]
    cosine = jnp.cos(angles)
    sine = jnp.sin(angles)
    sine = jnp.where(lane < HALF, -sine, sine)
    load_q.wait()

    def rotate(plane, target, index, carry):
        head = (index // HEADS * 2 + plane) * HEADS + lax.rem(index, HEADS)
        value = q_in[:, at(head, DH)].astype(jnp.float32)
        swapped = pltpu.roll(value, HALF, axis=1)
        turned = (value * cosine + swapped * sine).astype(jnp.bfloat16)
        for slot in range(SLOTS):
            target[slot, :, at(index, DH)] = turned[slot * TILE:(slot + 1) * TILE, :]
        return carry

    mine = q_chip.at[pl.ds(core * SLOTS, SLOTS)]
    lax.fori_loop(0, CHIPS * HEADS, functools.partial(rotate, 1 - core, q_out), 0)
    twin = remote(q_out, mine, twin_ssem.at[0], twin_rsem.at[0], seq=chip * 2 + 1 - core)
    twin.start()
    lax.fori_loop(0, CHIPS * HEADS, functools.partial(rotate, core, mine), 0)

    for offset in order:
        send_count(offset).wait_recv()
    to_scalar = pltpu.make_async_copy(count_all, counts, local_sem.at[3])
    to_scalar.start()
    to_scalar.wait()

    def count_of(offset, which):
        return counts[lax.rem(chip + offset, CHIPS) * 2 + which, 0, 0]

    first_core = [count_of(offset, 0) for offset in range(CHIPS)]
    there = [first_core[offset] + count_of(offset, 1) for offset in range(CHIPS)]
    below, above, by_a, by_b, total = [], [], [], [], []
    misfit = jnp.int32(0)
    for to in range(CHIPS):
        near_a, near_b = [jnp.int32(0)], [jnp.int32(0)]
        for away in range(1, CHIPS):
            near_a.append(near_a[-1] + there[(to - away) % CHIPS])
            near_b.append(near_b[-1] + there[(to + away) % CHIPS])
        whole = near_a[-1]
        fit_a = fit_b = whole
        for away in range(1, CHIPS):
            fit_a = jnp.minimum(fit_a, near_a[away - 1] + ROOM[away])
            fit_b = jnp.minimum(fit_b, near_b[away - 1] + ROOM[away])
        misfit = jnp.maximum(misfit, whole - fit_a - fit_b)
        below.append(near_a)
        above.append(near_b)
        by_a.append(fit_a)
        by_b.append(whole - fit_a)
        total.append(whole)

    flag_ref[0] = misfit

    def tile_at(rank):
        index = jnp.where(rank < first_core[0], rank, rank + SLOTS - first_core[0])
        return jnp.clip(index, 0, 2 * SLOTS - 1)

    def hop_a(hops):
        return remote(pack_a.at[pl.ds(hops * 8, ROOM[hops])], land_a.at[pl.ds(hops * 8, ROOM[hops])],
                      hop_ssem.at[0, hops], hop_rsem.at[0, hops], seq=peer(2))

    def hop_b(hops):
        return remote(pack_b.at[pl.ds(hops * 8, ROOM[hops])], land_b.at[pl.ds(hops * 8, ROOM[hops])],
                      hop_ssem.at[1, hops], hop_rsem.at[1, hops], seq=peer(N - 2))

    twin.wait_recv()
    for hops in range(HOPS, 0, -1):
        if hops < HOPS:
            hop_a(hops + 1).wait_recv()
            hop_b(hops + 1).wait_recv()
        to_a, to_b = hops, CHIPS - hops
        column_a = at(lax.rem(chip + to_a, CHIPS), LOCAL)
        column_b = at(lax.rem(chip + to_b, CHIPS), LOCAL)
        for slot in range(ROOM[hops]):
            rank = by_a[to_a] - 1 - slot - below[to_a][hops - 1]
            value = q_chip[tile_at(rank), :, column_a]
            if slot < ROOM[hops + 1]:
                is_mine = jnp.logical_and(rank >= 0, rank < there[0])
                value = jnp.where(is_mine, value, land_a[(hops + 1) * 8 + slot])
            pack_a[hops * 8 + slot] = value
            rank = by_b[to_b] - 1 - slot - above[to_b][hops - 1]
            value = q_chip[tile_at(there[0] - 1 - rank), :, column_b]
            if slot < ROOM[hops + 1]:
                is_mine = jnp.logical_and(rank >= 0, rank < there[0])
                value = jnp.where(is_mine, value, land_b[(hops + 1) * 8 + slot])
            pack_b[hops * 8 + slot] = value
        hop_a(hops).start()
        hop_b(hops).start()
        start_bulk(PACE[HOPS + 1 - hops])
    start_bulk(len(bulk) - started)

    hop_a(1).wait_recv()
    hop_b(1).wait_recv()
    column = at(chip, LOCAL)
    for slot in range(LIVE):
        value = q_chip[tile_at(slot - total[0]), :, column]
        other = land_b[8 + jnp.clip(slot - by_a[0], 0, 7)]
        value = jnp.where(slot < total[0], other, value)
        if slot < ROOM[1]:
            value = jnp.where(slot < by_a[0], land_a[8 + slot], value)
        q_live[slot * TILE:(slot + 1) * TILE, :] = value

    own_k.wait()
    for offset in order:
        send_k(offset).wait_recv()

    factor = math.log2(math.e) / math.sqrt(DH)
    block = 2 * TILE

    def score(index, carry):
        for head in range(HEADS):
            columns = pl.ds(head * DH, DH)
            logits = lax.dot_general(
                q_live[at(index, block), columns], k_all[:, columns],
                (((1,), (1,)), ((), ())), preferred_element_type=jnp.float32,
            )
            largest = jnp.max(logits, axis=1, keepdims=True)
            weight = jnp.exp2((logits - largest) * factor)
            norm[at(index, block), columns] = jnp.broadcast_to(
                1.0 / jnp.sum(weight, axis=1, keepdims=True), (block, DH)
            )
            probs[head, at(index, block), :] = weight.astype(jnp.bfloat16)
        return carry

    lax.fori_loop(0, LIVE * TILE // block, score, 0)

    own_v.wait()
    for head in range(HEADS):
        columns = pl.ds(head * DH, DH)
        for offset in order:
            send_v(head, offset).wait_recv()

        def combine(index, carry):
            product = jnp.dot(
                probs[head, at(index, block), :], v_all[:, columns], preferred_element_type=jnp.float32
            )
            product = (product * norm[at(index, block), columns]).astype(jnp.bfloat16)
            for part in range(2):
                o_live[head, index * 2 + part] = product[part * TILE:(part + 1) * TILE, :]
            return carry

        lax.fori_loop(0, LIVE * TILE // block, combine, 0)
        for offset in order + [0]:
            home = peer(offset)
            away = lax.rem(home // 2 - chip + CHIPS, CHIPS)
            which = lax.rem(home, 2)
            back = (CHIPS - away)
            before = jnp.int32(0)
            for step in range(1, CHIPS):
                before = jnp.where(back == step, below[0][step - 1], before)
            rank = jnp.where(which == 0, 0, counts[home // 2 * 2, 0, 0])
            for slot in range(SLOTS):
                index = before + rank + slot
                index = jnp.where(index < by_a[0], by_a[0] - 1 - index, index)
                index = jnp.where(back == CHIPS, total[0] + rank + slot, index)
                o_send[offset, slot * TILE:(slot + 1) * TILE, columns] = o_live[head, jnp.clip(index, 0, LIVE - 1)]
            if offset > 0:
                send_o(head, offset).start()
    o_ref[:, at(me, LOCAL)] = o_send[0]

    for offset in order:
        send_count(offset).wait_send()
    twin.wait_send()
    for hops in range(1, HOPS + 1):
        hop_a(hops).wait_send()
        hop_b(hops).wait_send()
    for copy in bulk:
        copy.wait_send()
    for head in range(HEADS):
        for offset in order:
            send_o(head, offset).wait()
    for slot in range(SLOTS):
        rows = pl.ds(slot * TILE, TILE)
        o_ref[rows, :] = jnp.where(tiles_ref[0, slot] >= 0, o_ref[rows, :], jnp.zeros((), jnp.bfloat16))


def refresh(q_slots, k_cache, v_cache, tiles):
    width = q_slots.shape[1]
    inverse = 10000.0 ** (-np.arange(HALF) / HALF)
    inverse = jnp.asarray(np.broadcast_to(np.tile(inverse, 2)[None, :], (8, DH)), jnp.float32)
    dma = pltpu.SemaphoreType.DMA
    bf16, i32 = jnp.bfloat16, jnp.int32
    unit = (TILE, LOCAL)
    return pl.pallas_call(
        kernel,
        out_shape=(
            jax.ShapeDtypeStruct((ROWS, width), bf16),
            jax.ShapeDtypeStruct((1,), i32),
        ),
        in_specs=[
            pl.BlockSpec(memory_space=pltpu.SMEM),
            pl.BlockSpec(memory_space=pltpu.VMEM),
            pl.BlockSpec(memory_space=pl.ANY),
            pl.BlockSpec(memory_space=pl.ANY),
            pl.BlockSpec(memory_space=pl.ANY),
        ],
        out_specs=(pl.BlockSpec(memory_space=pltpu.VMEM), pl.BlockSpec(memory_space=pltpu.SMEM)),
        scratch_shapes=[
            pltpu.VMEM((ROWS, width), bf16),
            pltpu.VMEM((SLOTS, TILE, width // 2), bf16),
            pltpu.VMEM((2 * SLOTS, TILE, width // 2), bf16),
            pltpu.VMEM((LIVE * TILE, LOCAL), bf16),
            pltpu.VMEM((N * ROWS, LOCAL), bf16),
            pltpu.VMEM((N * ROWS, LOCAL), bf16),
            pltpu.VMEM((HEADS, LIVE * TILE, N * ROWS), bf16),
            pltpu.VMEM((LIVE * TILE, LOCAL), jnp.float32),
            pltpu.VMEM((HEADS, LIVE, TILE, DH), bf16),
            pltpu.VMEM((N, ROWS, LOCAL), bf16),
            pltpu.VMEM((8, DH), i32),
            pltpu.VMEM((N, 8, DH), i32),
            pltpu.SMEM((N, 8, DH), i32),
            pltpu.VMEM(((HOPS + 1) * 8,) + unit, bf16),
            pltpu.VMEM(((HOPS + 1) * 8,) + unit, bf16),
            pltpu.VMEM(((HOPS + 1) * 8,) + unit, bf16),
            pltpu.VMEM(((HOPS + 1) * 8,) + unit, bf16),
            dma((4,)),
            dma((N,)), dma((N,)),
            dma((1,)), dma((1,)),
            dma((2, HOPS + 1)), dma((2, HOPS + 1)),
            dma((N,)), dma((N,)),
            dma((HEADS, N)), dma((HEADS, N)),
            dma((HEADS, N)), dma((HEADS, N)),
        ],
        name="refresh_attention",
        compiler_params=pltpu.CompilerParams(
            collective_id=0, has_side_effects=True, vmem_limit_bytes=56 * 2**20
        ),
    )(tiles, inverse, q_slots, k_cache, v_cache)


def keep_live(attended, tiles):
    row = lax.broadcasted_iota(jnp.int32, attended.shape, 0)
    tile = jnp.where(row < TILE, tiles[0, 0], tiles[0, 1])
    return jnp.where(tile >= 0, attended, jnp.zeros((), attended.dtype))


def every_slot(q_slots, k_cache, v_cache, tiles):
    width = q_slots.shape[1]
    exchange = functools.partial(lax.all_to_all, axis_name="seq", tiled=True)
    keys = exchange(k_cache, split_axis=1, concat_axis=0)
    values = exchange(v_cache, split_axis=1, concat_axis=0)
    tile = lax.axis_index("seq") * SLOTS + jnp.maximum(tiles[0], 0)
    position = (tile[:, None] * TILE + jnp.arange(TILE, dtype=jnp.int32)).reshape(ROWS, 1, 1).astype(jnp.float32)
    angles = position * 10000.0 ** (-jnp.arange(HALF, dtype=jnp.float32) / HALF)
    cosine, sine = jnp.cos(angles), jnp.sin(angles)
    queries = q_slots.astype(jnp.float32).reshape(ROWS, width // DH, DH)
    a, b = queries[..., :HALF], queries[..., HALF:]
    rotated = jnp.concatenate([a * cosine - b * sine, b * cosine + a * sine], axis=-1)
    rotated = rotated.astype(jnp.bfloat16).reshape(ROWS, width)
    rotated = exchange(rotated, split_axis=1, concat_axis=0)

    def one(index):
        head = lax.rem(index, HEADS)
        rows = lax.dynamic_slice(rotated, (index // HEADS * 512, head * DH), (512, DH))
        head_keys = lax.dynamic_slice_in_dim(keys, head * DH, DH, 1)
        head_values = lax.dynamic_slice_in_dim(values, head * DH, DH, 1)
        logits = jnp.dot(rows, head_keys.T, preferred_element_type=jnp.float32) * DH**-0.5
        weight = jnp.exp(logits - jnp.max(logits, axis=-1, keepdims=True))
        weight = (weight / jnp.sum(weight, axis=-1, keepdims=True)).astype(jnp.bfloat16)
        return jnp.dot(weight, head_values, preferred_element_type=jnp.float32).astype(jnp.bfloat16)

    result = lax.map(one, jnp.arange(N * ROWS // 512 * HEADS))
    result = result.reshape(N * ROWS // 512, HEADS, 512, DH).swapaxes(1, 2).reshape(N * ROWS, LOCAL)
    return keep_live(exchange(result, split_axis=0, concat_axis=1), tiles)


def on_device(q_slots, k_cache, v_cache, tiles):
    attended, misfit = refresh(q_slots, k_cache, v_cache, tiles)
    def other_way(carry):
        rowwise = Layout(major_to_minor=(0, 1))
        _, *given = lax.optimization_barrier((carry[0], q_slots, k_cache, v_cache, tiles))
        given = [with_layout_constraint(array, rowwise) for array in given]
        return jnp.int32(0), with_layout_constraint(every_slot(*given), rowwise)

    return lax.while_loop(lambda carry: carry[0] > 0, other_way, (misfit[0], attended))[1]


def solution(mesh):
    spec = P(("req", "seq"), None)
    return jax.shard_map(
        on_device, mesh=mesh, in_specs=(spec,) * 4, out_specs=spec, check_vma=False
    )
```

```python
import functools
import math

import jax
import jax.numpy as jnp
import numpy as np
from jax import lax
from jax.experimental import pallas as pl
from jax.experimental.layout import Layout, with_layout_constraint
from jax.experimental.pallas import tpu as pltpu
from jax.sharding import PartitionSpec as P

MESH = pl.DeviceIdType.MESH
DH = 128
HALF = DH // 2
TILE = 64
SLOTS = 2
LIVE = 12
HEADS = 2
LOCAL = HEADS * DH
N = 16
CHIPS = N // 2
ROWS = SLOTS * TILE
ROOM = {1: 8, 2: 6, 3: 5, 4: 3, 5: 1, 6: 0, 7: 0}
HOPS = 5
PACE = (10, 1)


def kernel(tiles_ref, inv_ref, q_ref, k_ref, v_ref, o_ref, flag_ref,
           q_in, q_out, q_chip, q_live, k_all, v_all, probs, norm, o_sum, o_live, o_send,
           count_out, count_all, counts,
           pack_a, pack_b, land_a, land_b,
           local_sem, count_ssem, count_rsem, twin_ssem, twin_rsem,
           hop_ssem, hop_rsem, k_ssem, k_rsem, v_ssem, v_rsem, o_ssem, o_rsem):
    me = lax.axis_index("seq")
    chip = me // 2
    core = lax.rem(me, 2)

    def at(index, size):
        return pl.ds(pl.multiple_of(index * size, size), size)

    def peer(offset):
        return lax.rem(me + offset, N)

    def remote(source, target, ssem, rsem, **where):
        return pltpu.make_async_remote_copy(
            src_ref=source, dst_ref=target, send_sem=ssem, recv_sem=rsem,
            device_id=where, device_id_type=MESH,
        )

    barrier = pltpu.get_barrier_semaphore()
    for offset in range(1, N):
        pl.semaphore_signal(barrier, inc=1, device_id={"seq": peer(offset)}, device_id_type=MESH)
    load_q = pltpu.make_async_copy(q_ref, q_in, local_sem.at[0])
    load_q.start()
    own_k = pltpu.make_async_copy(k_ref.at[:, at(me, LOCAL)], k_all.at[at(me, ROWS), :], local_sem.at[1])
    own_k.start()
    own_v = pltpu.make_async_copy(v_ref.at[:, at(me, LOCAL)], v_all.at[at(me, ROWS), :], local_sem.at[2])
    own_v.start()

    first_live = (tiles_ref[0, 0] >= 0).astype(jnp.int32)
    second_live = (tiles_ref[0, 1] >= 0).astype(jnp.int32)
    count = jnp.full((8, DH), first_live + second_live, jnp.int32)
    count_out[...] = count
    count_all[me] = count
    row = lax.broadcasted_iota(jnp.int32, (ROWS, DH), 0)
    lane = lax.broadcasted_iota(jnp.int32, (ROWS, DH), 1)
    first = jnp.maximum(tiles_ref[0, 0], 0) * TILE
    second = (jnp.maximum(tiles_ref[0, 1], 0) - 1) * TILE
    position = (me * ROWS + row + jnp.where(row < TILE, first, second)).astype(jnp.float32)
    angles = position * inv_ref[0:1, :]
    cosine = jnp.cos(angles)
    sine = jnp.sin(angles)
    sine = jnp.where(lane < HALF, -sine, sine)
    load_q.wait()

    def rotate(plane, target, index, carry):
        head = (index // HEADS * 2 + plane) * HEADS + lax.rem(index, HEADS)
        value = q_in[:, at(head, DH)].astype(jnp.float32)
        swapped = pltpu.roll(value, HALF, axis=1)
        turned = (value * cosine + swapped * sine).astype(jnp.bfloat16)
        for slot in range(SLOTS):
            target[slot, :, at(index, DH)] = turned[slot * TILE:(slot + 1) * TILE, :]
        return carry

    mine = q_chip.at[pl.ds(core * SLOTS, SLOTS)]
    lax.fori_loop(0, CHIPS * HEADS, functools.partial(rotate, 1 - core, q_out), 0)
    pl.semaphore_wait(barrier, N - 1)

    def send_count(offset):
        return remote(count_out, count_all.at[me], count_ssem.at[offset], count_rsem.at[offset], seq=peer(offset))

    def send_k(offset):
        to = peer(offset)
        return remote(k_ref.at[:, at(to, LOCAL)], k_all.at[at(me, ROWS), :],
                      k_ssem.at[offset], k_rsem.at[offset], seq=to)

    def send_v(head, offset):
        to = peer(offset)
        return remote(v_ref.at[:, at(to * HEADS + head, DH)], v_all.at[at(me, ROWS), pl.ds(head * DH, DH)],
                      v_ssem.at[head, offset], v_rsem.at[head, offset], seq=to)

    def send_o(head, offset):
        to = peer(offset)
        return remote(o_send.at[offset, :, pl.ds(head * DH, DH)], o_ref.at[:, at(me * HEADS + head, DH)],
                      o_ssem.at[head, offset], o_rsem.at[head, offset], seq=to)

    order = []
    for step in range(1, N // 2 + 1):
        order += [step] if step == N // 2 else [step, N - step]
    bulk = [send_k(offset) for offset in order]
    bulk += [send_v(head, offset) for head in range(HEADS) for offset in order]
    started = 0

    def start_bulk(amount):
        nonlocal started
        for copy in bulk[started:started + amount]:
            copy.start()
        started += amount

    for offset in order:
        send_count(offset).start()
    twin = remote(q_out, mine, twin_ssem.at[0], twin_rsem.at[0], seq=chip * 2 + 1 - core)
    twin.start()
    start_bulk(PACE[0])

    lax.fori_loop(0, CHIPS * HEADS, functools.partial(rotate, core, mine), 0)

    for offset in order:
        send_count(offset).wait_recv()
    to_scalar = pltpu.make_async_copy(count_all, counts, local_sem.at[3])
    to_scalar.start()
    to_scalar.wait()

    def count_of(offset, which):
        return counts[lax.rem(chip + offset, CHIPS) * 2 + which, 0, 0]

    first_core = [count_of(offset, 0) for offset in range(CHIPS)]
    there = [first_core[offset] + count_of(offset, 1) for offset in range(CHIPS)]
    below, above, by_a, by_b, total = [], [], [], [], []
    misfit = jnp.int32(0)
    for to in range(CHIPS):
        near_a, near_b = [jnp.int32(0)], [jnp.int32(0)]
        for away in range(1, CHIPS):
            near_a.append(near_a[-1] + there[(to - away) % CHIPS])
            near_b.append(near_b[-1] + there[(to + away) % CHIPS])
        whole = near_a[-1]
        fit_a = fit_b = whole
        for away in range(1, CHIPS):
            fit_a = jnp.minimum(fit_a, near_a[away - 1] + ROOM[away])
            fit_b = jnp.minimum(fit_b, near_b[away - 1] + ROOM[away])
        misfit = jnp.maximum(misfit, whole - fit_a - fit_b)
        below.append(near_a)
        above.append(near_b)
        by_a.append(fit_a)
        by_b.append(whole - fit_a)
        total.append(whole)

    flag_ref[0] = misfit

    def tile_at(rank):
        index = jnp.where(rank < first_core[0], rank, rank + SLOTS - first_core[0])
        return jnp.clip(index, 0, 2 * SLOTS - 1)

    def hop(side, hops, head):
        pack, land, to = ((pack_a, land_a, 2), (pack_b, land_b, N - 2))[side]
        slots = pl.ds(hops * 8, ROOM[hops])
        return remote(pack.at[head, slots], land.at[head, slots], hop_ssem.at[side, hops, head],
                      hop_rsem.at[side, hops, head], seq=peer(to))

    twin.wait_recv()
    for hops in range(HOPS, 0, -1):
        to_a, to_b = hops, CHIPS - hops
        for head in range(HEADS):
            if hops < HOPS:
                hop(0, hops + 1, head).wait_recv()
                hop(1, hops + 1, head).wait_recv()
            column_a = at(lax.rem(chip + to_a, CHIPS) * HEADS + head, DH)
            column_b = at(lax.rem(chip + to_b, CHIPS) * HEADS + head, DH)
            for slot in range(ROOM[hops]):
                rank = by_a[to_a] - 1 - slot - below[to_a][hops - 1]
                value = q_chip[tile_at(rank), :, column_a]
                if slot < ROOM[hops + 1]:
                    is_mine = jnp.logical_and(rank >= 0, rank < there[0])
                    value = jnp.where(is_mine, value, land_a[head, (hops + 1) * 8 + slot])
                pack_a[head, hops * 8 + slot] = value
                rank = by_b[to_b] - 1 - slot - above[to_b][hops - 1]
                value = q_chip[tile_at(there[0] - 1 - rank), :, column_b]
                if slot < ROOM[hops + 1]:
                    is_mine = jnp.logical_and(rank >= 0, rank < there[0])
                    value = jnp.where(is_mine, value, land_b[head, (hops + 1) * 8 + slot])
                pack_b[head, hops * 8 + slot] = value
            hop(0, hops, head).start()
            hop(1, hops, head).start()
            start_bulk(PACE[1])
    start_bulk(len(bulk) - started)

    for head in range(HEADS):
        hop(0, 1, head).wait_recv()
        hop(1, 1, head).wait_recv()
    for head in range(HEADS):
        column = at(chip * HEADS + head, DH)
        columns = pl.ds(head * DH, DH)
        for slot in range(LIVE):
            value = q_chip[tile_at(slot - total[0]), :, column]
            other = land_b[head, 8 + jnp.clip(slot - by_a[0], 0, 7)]
            value = jnp.where(slot < total[0], other, value)
            if slot < ROOM[1]:
                value = jnp.where(slot < by_a[0], land_a[head, 8 + slot], value)
            q_live[slot * TILE:(slot + 1) * TILE, columns] = value

    own_k.wait()
    for offset in order:
        send_k(offset).wait_recv()

    factor = math.log2(math.e) / math.sqrt(DH)
    block = 2 * TILE

    def score(index, carry):
        for head in range(HEADS):
            columns = pl.ds(head * DH, DH)
            logits = lax.dot_general(
                q_live[at(index, block), columns], k_all[:, columns],
                (((1,), (1,)), ((), ())), preferred_element_type=jnp.float32,
            )
            largest = jnp.max(logits, axis=1, keepdims=True)
            weight = jnp.exp2((logits - largest) * factor)
            norm[at(index, block), columns] = jnp.broadcast_to(
                1.0 / jnp.sum(weight, axis=1, keepdims=True), (block, DH)
            )
            probs[head, at(index, block), :] = weight.astype(jnp.bfloat16)
        return carry

    lax.fori_loop(0, LIVE * TILE // block, score, 0)

    places = {}
    for offset in order + [0]:
        home = peer(offset)
        back = CHIPS - lax.rem(home // 2 - chip + CHIPS, CHIPS)
        before = jnp.int32(0)
        for step in range(1, CHIPS):
            before = jnp.where(back == step, below[0][step - 1], before)
        rank = jnp.where(lax.rem(home, 2) == 0, 0, counts[home // 2 * 2, 0, 0])
        for slot in range(SLOTS):
            index = before + rank + slot
            index = jnp.where(index < by_a[0], by_a[0] - 1 - index, index)
            index = jnp.where(back == CHIPS, total[0] + rank + slot, index)
            places[offset, slot] = jnp.clip(index, 0, LIVE - 1)

    own_v.wait()
    for head in range(HEADS):
        columns = pl.ds(head * DH, DH)
        for step, away in enumerate((0, 1, 7, 2, 6, 3, 5, 4)):
            if away == 0:
                send_v(head, lax.rem(N + 2 * core - 1, N)).wait_recv()
            else:
                for which in range(2):
                    send_v(head, 2 * away + core - which).wait_recv()
            rows = at(lax.rem(chip - away + CHIPS, CHIPS), 2 * ROWS)
            product = jnp.dot(probs[head, :, rows], v_all[rows, columns], preferred_element_type=jnp.float32)
            if step == 0:
                o_sum[...] = product
            elif step < CHIPS - 1:
                o_sum[...] += product
            else:
                product = ((o_sum[...] + product) * norm[:, columns]).astype(jnp.bfloat16)
                for slot in range(LIVE):
                    o_live[head, slot] = product[slot * TILE:(slot + 1) * TILE, :]
        for offset in order + [0]:
            for slot in range(SLOTS):
                o_send[offset, slot * TILE:(slot + 1) * TILE, columns] = o_live[head, places[offset, slot]]
            if offset > 0:
                send_o(head, offset).start()
    o_ref[:, at(me, LOCAL)] = o_send[0]

    for offset in order:
        send_count(offset).wait_send()
    twin.wait_send()
    for hops in range(1, HOPS + 1):
        for head in range(HEADS):
            hop(0, hops, head).wait_send()
            hop(1, hops, head).wait_send()
    for copy in bulk:
        copy.wait_send()
    for head in range(HEADS):
        for offset in order:
            send_o(head, offset).wait()
    for slot in range(SLOTS):
        rows = pl.ds(slot * TILE, TILE)
        o_ref[rows, :] = jnp.where(tiles_ref[0, slot] >= 0, o_ref[rows, :], jnp.zeros((), jnp.bfloat16))


def refresh(q_slots, k_cache, v_cache, tiles):
    width = q_slots.shape[1]
    inverse = 10000.0 ** (-np.arange(HALF) / HALF)
    inverse = jnp.asarray(np.broadcast_to(np.tile(inverse, 2)[None, :], (8, DH)), jnp.float32)
    dma = pltpu.SemaphoreType.DMA
    bf16, i32 = jnp.bfloat16, jnp.int32
    packets = pltpu.VMEM((HEADS, (HOPS + 1) * 8, TILE, DH), bf16)
    return pl.pallas_call(
        kernel,
        out_shape=(
            jax.ShapeDtypeStruct((ROWS, width), bf16),
            jax.ShapeDtypeStruct((1,), i32),
        ),
        in_specs=[
            pl.BlockSpec(memory_space=pltpu.SMEM),
            pl.BlockSpec(memory_space=pltpu.VMEM),
            pl.BlockSpec(memory_space=pl.ANY),
            pl.BlockSpec(memory_space=pl.ANY),
            pl.BlockSpec(memory_space=pl.ANY),
        ],
        out_specs=(pl.BlockSpec(memory_space=pltpu.VMEM), pl.BlockSpec(memory_space=pltpu.SMEM)),
        scratch_shapes=[
            pltpu.VMEM((ROWS, width), bf16),
            pltpu.VMEM((SLOTS, TILE, width // 2), bf16),
            pltpu.VMEM((2 * SLOTS, TILE, width // 2), bf16),
            pltpu.VMEM((LIVE * TILE, LOCAL), bf16),
            pltpu.VMEM((N * ROWS, LOCAL), bf16),
            pltpu.VMEM((N * ROWS, LOCAL), bf16),
            pltpu.VMEM((HEADS, LIVE * TILE, N * ROWS), bf16),
            pltpu.VMEM((LIVE * TILE, LOCAL), jnp.float32),
            pltpu.VMEM((LIVE * TILE, DH), jnp.float32),
            pltpu.VMEM((HEADS, LIVE, TILE, DH), bf16),
            pltpu.VMEM((N, ROWS, LOCAL), bf16),
            pltpu.VMEM((8, DH), i32),
            pltpu.VMEM((N, 8, DH), i32),
            pltpu.SMEM((N, 8, DH), i32),
            packets, packets, packets, packets,
            dma((4,)),
            dma((N,)), dma((N,)),
            dma((1,)), dma((1,)),
            dma((2, HOPS + 1, HEADS)), dma((2, HOPS + 1, HEADS)),
            dma((N,)), dma((N,)),
            dma((HEADS, N)), dma((HEADS, N)),
            dma((HEADS, N)), dma((HEADS, N)),
        ],
        name="refresh_attention",
        compiler_params=pltpu.CompilerParams(
            collective_id=0, has_side_effects=True, vmem_limit_bytes=56 * 2**20
        ),
    )(tiles, inverse, q_slots, k_cache, v_cache)


def keep_live(attended, tiles):
    row = lax.broadcasted_iota(jnp.int32, attended.shape, 0)
    tile = jnp.where(row < TILE, tiles[0, 0], tiles[0, 1])
    return jnp.where(tile >= 0, attended, jnp.zeros((), attended.dtype))


def every_slot(q_slots, k_cache, v_cache, tiles):
    width = q_slots.shape[1]
    exchange = functools.partial(lax.all_to_all, axis_name="seq", tiled=True)
    keys = exchange(k_cache, split_axis=1, concat_axis=0)
    values = exchange(v_cache, split_axis=1, concat_axis=0)
    tile = lax.axis_index("seq") * SLOTS + jnp.maximum(tiles[0], 0)
    position = (tile[:, None] * TILE + jnp.arange(TILE, dtype=jnp.int32)).reshape(ROWS, 1, 1).astype(jnp.float32)
    angles = position * 10000.0 ** (-jnp.arange(HALF, dtype=jnp.float32) / HALF)
    cosine, sine = jnp.cos(angles), jnp.sin(angles)
    queries = q_slots.astype(jnp.float32).reshape(ROWS, width // DH, DH)
    a, b = queries[..., :HALF], queries[..., HALF:]
    rotated = jnp.concatenate([a * cosine - b * sine, b * cosine + a * sine], axis=-1)
    rotated = rotated.astype(jnp.bfloat16).reshape(ROWS, width)
    rotated = exchange(rotated, split_axis=1, concat_axis=0)

    def one(index):
        head = lax.rem(index, HEADS)
        rows = lax.dynamic_slice(rotated, (index // HEADS * 512, head * DH), (512, DH))
        head_keys = lax.dynamic_slice_in_dim(keys, head * DH, DH, 1)
        head_values = lax.dynamic_slice_in_dim(values, head * DH, DH, 1)
        logits = jnp.dot(rows, head_keys.T, preferred_element_type=jnp.float32) * DH**-0.5
        weight = jnp.exp(logits - jnp.max(logits, axis=-1, keepdims=True))
        weight = (weight / jnp.sum(weight, axis=-1, keepdims=True)).astype(jnp.bfloat16)
        return jnp.dot(weight, head_values, preferred_element_type=jnp.float32).astype(jnp.bfloat16)

    result = lax.map(one, jnp.arange(N * ROWS // 512 * HEADS))
    result = result.reshape(N * ROWS // 512, HEADS, 512, DH).swapaxes(1, 2).reshape(N * ROWS, LOCAL)
    return keep_live(exchange(result, split_axis=0, concat_axis=1), tiles)


def on_device(q_slots, k_cache, v_cache, tiles):
    attended, misfit = refresh(q_slots, k_cache, v_cache, tiles)
    def other_way():
        rowwise = Layout(major_to_minor=(0, 1))
        given = [with_layout_constraint(array, rowwise) for array in (q_slots, k_cache, v_cache, tiles)]
        return with_layout_constraint(every_slot(*given), rowwise)

    return lax.cond(misfit[0] > 0, other_way, lambda: attended)


def solution(mesh):
    spec = P(("req", "seq"), None)
    return jax.shard_map(
        on_device, mesh=mesh, in_specs=(spec,) * 4, out_specs=spec, check_vma=False
    )
```

```python
import functools
import math

import jax
import jax.numpy as jnp
import numpy as np
from jax import lax
from jax.experimental import pallas as pl
from jax.experimental.layout import Layout, with_layout_constraint
from jax.experimental.pallas import tpu as pltpu
from jax.sharding import PartitionSpec as P

MESH = pl.DeviceIdType.MESH
DH = 128
HALF = DH // 2
TILE = 64
SLOTS = 2
LIVE = 12
HEADS = 2
LOCAL = HEADS * DH
N = 16
CHIPS = N // 2
ROWS = SLOTS * TILE
ROOM = {1: 8, 2: 6, 3: 5, 4: 3, 5: 1, 6: 0, 7: 0}
HOPS = 5
PACE = (10, 1)


def kernel(tiles_in, inv_in, q_ref, k_ref, v_ref, o_ref, flag_ref,
           tiles_ref, inv_ref, q_in, q_out, q_chip, q_live, k_all, v_all, probs, norm, o_sum, o_live, o_send,
           count_out, count_all, counts,
           pack_a, pack_b, land_a, land_b,
           local_sem, count_ssem, count_rsem, twin_ssem, twin_rsem,
           hop_ssem, hop_rsem, k_ssem, k_rsem, v_ssem, v_rsem, o_ssem, o_rsem):
    me = lax.axis_index("seq")
    chip = me // 2
    core = lax.rem(me, 2)

    def at(index, size):
        return pl.ds(pl.multiple_of(index * size, size), size)

    def peer(offset):
        return lax.rem(me + offset, N)

    def remote(source, target, ssem, rsem, **where):
        return pltpu.make_async_remote_copy(
            src_ref=source, dst_ref=target, send_sem=ssem, recv_sem=rsem,
            device_id=where, device_id_type=MESH,
        )

    barrier = pltpu.get_barrier_semaphore()
    for offset in range(1, N):
        pl.semaphore_signal(barrier, inc=1, device_id={"seq": peer(offset)}, device_id_type=MESH)
    load_tiles = pltpu.make_async_copy(tiles_in, tiles_ref, local_sem.at[4])
    load_tiles.start()
    load_inv = pltpu.make_async_copy(inv_in, inv_ref, local_sem.at[5])
    load_inv.start()
    load_q = pltpu.make_async_copy(q_ref, q_in, local_sem.at[0])
    load_q.start()
    own_k = pltpu.make_async_copy(k_ref.at[:, at(me, LOCAL)], k_all.at[at(me, ROWS), :], local_sem.at[1])
    own_k.start()
    own_v = pltpu.make_async_copy(v_ref.at[:, at(me, LOCAL)], v_all.at[at(me, ROWS), :], local_sem.at[2])
    own_v.start()

    load_tiles.wait()
    first_live = (tiles_ref[0, 0] >= 0).astype(jnp.int32)
    second_live = (tiles_ref[0, 1] >= 0).astype(jnp.int32)
    count = jnp.full((8, DH), first_live + second_live, jnp.int32)
    count_out[...] = count
    count_all[me] = count
    row = lax.broadcasted_iota(jnp.int32, (ROWS, DH), 0)
    lane = lax.broadcasted_iota(jnp.int32, (ROWS, DH), 1)
    first = jnp.maximum(tiles_ref[0, 0], 0) * TILE
    second = (jnp.maximum(tiles_ref[0, 1], 0) - 1) * TILE
    position = (me * ROWS + row + jnp.where(row < TILE, first, second)).astype(jnp.float32)
    load_inv.wait()
    angles = position * inv_ref[0:1, :]
    cosine = jnp.cos(angles)
    sine = jnp.sin(angles)
    sine = jnp.where(lane < HALF, -sine, sine)
    load_q.wait()

    def rotate(plane, target, index, carry):
        head = (index // HEADS * 2 + plane) * HEADS + lax.rem(index, HEADS)
        value = q_in[:, at(head, DH)].astype(jnp.float32)
        swapped = pltpu.roll(value, HALF, axis=1)
        turned = (value * cosine + swapped * sine).astype(jnp.bfloat16)
        for slot in range(SLOTS):
            target[slot, :, at(index, DH)] = turned[slot * TILE:(slot + 1) * TILE, :]
        return carry

    mine = q_chip.at[pl.ds(core * SLOTS, SLOTS)]
    lax.fori_loop(0, CHIPS * HEADS, functools.partial(rotate, 1 - core, q_out), 0)
    pl.semaphore_wait(barrier, N - 1)

    def send_count(offset):
        return remote(count_out, count_all.at[me], count_ssem.at[offset], count_rsem.at[offset], seq=peer(offset))

    def send_k(offset):
        to = peer(offset)
        return remote(k_ref.at[:, at(to, LOCAL)], k_all.at[at(me, ROWS), :],
                      k_ssem.at[offset], k_rsem.at[offset], seq=to)

    def send_v(head, offset):
        to = peer(offset)
        return remote(v_ref.at[:, at(to * HEADS + head, DH)], v_all.at[at(me, ROWS), pl.ds(head * DH, DH)],
                      v_ssem.at[head, offset], v_rsem.at[head, offset], seq=to)

    def send_o(head, offset):
        to = peer(offset)
        return remote(o_send.at[offset, :, pl.ds(head * DH, DH)], o_ref.at[:, at(me * HEADS + head, DH)],
                      o_ssem.at[head, offset], o_rsem.at[head, offset], seq=to)

    order = []
    for step in range(1, N // 2 + 1):
        order += [step] if step == N // 2 else [step, N - step]
    bulk = [send_k(offset) for offset in order]
    bulk += [send_v(head, offset) for head in range(HEADS) for offset in order]
    started = 0

    def start_bulk(amount):
        nonlocal started
        for copy in bulk[started:started + amount]:
            copy.start()
        started += amount

    for offset in order:
        send_count(offset).start()
    twin = remote(q_out, mine, twin_ssem.at[0], twin_rsem.at[0], seq=chip * 2 + 1 - core)
    twin.start()
    start_bulk(PACE[0])

    lax.fori_loop(0, CHIPS * HEADS, functools.partial(rotate, core, mine), 0)

    for offset in order:
        send_count(offset).wait_recv()
    to_scalar = pltpu.make_async_copy(count_all, counts, local_sem.at[3])
    to_scalar.start()
    to_scalar.wait()

    def count_of(offset, which):
        return counts[lax.rem(chip + offset, CHIPS) * 2 + which, 0, 0]

    first_core = [count_of(offset, 0) for offset in range(CHIPS)]
    there = [first_core[offset] + count_of(offset, 1) for offset in range(CHIPS)]
    below, above, by_a, by_b, total = [], [], [], [], []
    misfit = jnp.int32(0)
    for to in range(CHIPS):
        near_a, near_b = [jnp.int32(0)], [jnp.int32(0)]
        for away in range(1, CHIPS):
            near_a.append(near_a[-1] + there[(to - away) % CHIPS])
            near_b.append(near_b[-1] + there[(to + away) % CHIPS])
        whole = near_a[-1]
        fit_a = fit_b = whole
        for away in range(1, CHIPS):
            fit_a = jnp.minimum(fit_a, near_a[away - 1] + ROOM[away])
            fit_b = jnp.minimum(fit_b, near_b[away - 1] + ROOM[away])
        misfit = jnp.maximum(misfit, whole - fit_a - fit_b)
        below.append(near_a)
        above.append(near_b)
        by_a.append(fit_a)
        by_b.append(whole - fit_a)
        total.append(whole)

    flag_ref[0] = misfit

    def tile_at(rank):
        index = jnp.where(rank < first_core[0], rank, rank + SLOTS - first_core[0])
        return jnp.clip(index, 0, 2 * SLOTS - 1)

    def hop(side, hops, head):
        pack, land, to = ((pack_a, land_a, 2), (pack_b, land_b, N - 2))[side]
        slots = pl.ds(hops * 8, ROOM[hops])
        return remote(pack.at[head, slots], land.at[head, slots], hop_ssem.at[side, hops, head],
                      hop_rsem.at[side, hops, head], seq=peer(to))

    twin.wait_recv()
    for hops in range(HOPS, 0, -1):
        to_a, to_b = hops, CHIPS - hops
        for head in range(HEADS):
            if hops < HOPS:
                hop(0, hops + 1, head).wait_recv()
                hop(1, hops + 1, head).wait_recv()
            column_a = at(lax.rem(chip + to_a, CHIPS) * HEADS + head, DH)
            column_b = at(lax.rem(chip + to_b, CHIPS) * HEADS + head, DH)
            for slot in range(ROOM[hops]):
                rank = by_a[to_a] - 1 - slot - below[to_a][hops - 1]
                value = q_chip[tile_at(rank), :, column_a]
                if slot < ROOM[hops + 1]:
                    is_mine = jnp.logical_and(rank >= 0, rank < there[0])
                    value = jnp.where(is_mine, value, land_a[head, (hops + 1) * 8 + slot])
                pack_a[head, hops * 8 + slot] = value
                rank = by_b[to_b] - 1 - slot - above[to_b][hops - 1]
                value = q_chip[tile_at(there[0] - 1 - rank), :, column_b]
                if slot < ROOM[hops + 1]:
                    is_mine = jnp.logical_and(rank >= 0, rank < there[0])
                    value = jnp.where(is_mine, value, land_b[head, (hops + 1) * 8 + slot])
                pack_b[head, hops * 8 + slot] = value
            hop(0, hops, head).start()
            hop(1, hops, head).start()
            start_bulk(PACE[1])
    start_bulk(len(bulk) - started)

    for head in range(HEADS):
        hop(0, 1, head).wait_recv()
        hop(1, 1, head).wait_recv()
    for head in range(HEADS):
        column = at(chip * HEADS + head, DH)
        columns = pl.ds(head * DH, DH)
        for slot in range(LIVE):
            value = q_chip[tile_at(slot - total[0]), :, column]
            other = land_b[head, 8 + jnp.clip(slot - by_a[0], 0, 7)]
            value = jnp.where(slot < total[0], other, value)
            if slot < ROOM[1]:
                value = jnp.where(slot < by_a[0], land_a[head, 8 + slot], value)
            q_live[slot * TILE:(slot + 1) * TILE, columns] = value

    own_k.wait()
    for offset in order:
        send_k(offset).wait_recv()

    factor = math.log2(math.e) / math.sqrt(DH)
    block = 2 * TILE

    def score(index, carry):
        for head in range(HEADS):
            columns = pl.ds(head * DH, DH)
            logits = lax.dot_general(
                q_live[at(index, block), columns], k_all[:, columns],
                (((1,), (1,)), ((), ())), preferred_element_type=jnp.float32,
            )
            largest = jnp.max(logits, axis=1, keepdims=True)
            weight = jnp.exp2((logits - largest) * factor)
            norm[at(index, block), columns] = jnp.broadcast_to(
                1.0 / jnp.sum(weight, axis=1, keepdims=True), (block, DH)
            )
            probs[head, at(index, block), :] = weight.astype(jnp.bfloat16)
        return carry

    lax.fori_loop(0, LIVE * TILE // block, score, 0)

    places = {}
    for offset in order + [0]:
        home = peer(offset)
        back = CHIPS - lax.rem(home // 2 - chip + CHIPS, CHIPS)
        before = jnp.int32(0)
        for step in range(1, CHIPS):
            before = jnp.where(back == step, below[0][step - 1], before)
        rank = jnp.where(lax.rem(home, 2) == 0, 0, counts[home // 2 * 2, 0, 0])
        for slot in range(SLOTS):
            index = before + rank + slot
            index = jnp.where(index < by_a[0], by_a[0] - 1 - index, index)
            index = jnp.where(back == CHIPS, total[0] + rank + slot, index)
            places[offset, slot] = jnp.clip(index, 0, LIVE - 1)

    own_v.wait()
    for head in range(HEADS):
        columns = pl.ds(head * DH, DH)
        for step, away in enumerate((0, 1, 7, 2, 6, 3, 5, 4)):
            if away == 0:
                send_v(head, lax.rem(N + 2 * core - 1, N)).wait_recv()
            else:
                for which in range(2):
                    send_v(head, 2 * away + core - which).wait_recv()
            rows = at(lax.rem(chip - away + CHIPS, CHIPS), 2 * ROWS)
            product = jnp.dot(probs[head, :, rows], v_all[rows, columns], preferred_element_type=jnp.float32)
            if step == 0:
                o_sum[...] = product
            elif step < CHIPS - 1:
                o_sum[...] += product
            else:
                product = ((o_sum[...] + product) * norm[:, columns]).astype(jnp.bfloat16)
                for slot in range(LIVE):
                    o_live[head, slot] = product[slot * TILE:(slot + 1) * TILE, :]
        for offset in order + [0]:
            for slot in range(SLOTS):
                o_send[offset, slot * TILE:(slot + 1) * TILE, columns] = o_live[head, places[offset, slot]]
            if offset > 0:
                send_o(head, offset).start()
    o_ref[:, at(me, LOCAL)] = o_send[0]

    for offset in order:
        send_count(offset).wait_send()
    twin.wait_send()
    for hops in range(1, HOPS + 1):
        for head in range(HEADS):
            hop(0, hops, head).wait_send()
            hop(1, hops, head).wait_send()
    for copy in bulk:
        copy.wait_send()
    for head in range(HEADS):
        for offset in order:
            send_o(head, offset).wait()
    for slot in range(SLOTS):
        rows = pl.ds(slot * TILE, TILE)
        o_ref[rows, :] = jnp.where(tiles_ref[0, slot] >= 0, o_ref[rows, :], jnp.zeros((), jnp.bfloat16))


def refresh(q_slots, k_cache, v_cache, tiles):
    width = q_slots.shape[1]
    inverse = 10000.0 ** (-np.arange(HALF) / HALF)
    inverse = jnp.asarray(np.broadcast_to(np.tile(inverse, 2)[None, :], (8, DH)), jnp.float32)
    dma = pltpu.SemaphoreType.DMA
    bf16, i32 = jnp.bfloat16, jnp.int32
    packets = pltpu.VMEM((HEADS, (HOPS + 1) * 8, TILE, DH), bf16)
    return pl.pallas_call(
        kernel,
        out_shape=(
            jax.ShapeDtypeStruct((ROWS, width), bf16),
            jax.ShapeDtypeStruct((1,), i32),
        ),
        in_specs=[
            pl.BlockSpec(memory_space=pl.ANY),
            pl.BlockSpec(memory_space=pl.ANY),
            pl.BlockSpec(memory_space=pl.ANY),
            pl.BlockSpec(memory_space=pl.ANY),
            pl.BlockSpec(memory_space=pl.ANY),
        ],
        out_specs=(pl.BlockSpec(memory_space=pltpu.VMEM), pl.BlockSpec(memory_space=pltpu.SMEM)),
        scratch_shapes=[
            pltpu.SMEM((1, SLOTS), i32),
            pltpu.VMEM((8, DH), jnp.float32),
            pltpu.VMEM((ROWS, width), bf16),
            pltpu.VMEM((SLOTS, TILE, width // 2), bf16),
            pltpu.VMEM((2 * SLOTS, TILE, width // 2), bf16),
            pltpu.VMEM((LIVE * TILE, LOCAL), bf16),
            pltpu.VMEM((N * ROWS, LOCAL), bf16),
            pltpu.VMEM((N * ROWS, LOCAL), bf16),
            pltpu.VMEM((HEADS, LIVE * TILE, N * ROWS), bf16),
            pltpu.VMEM((LIVE * TILE, LOCAL), jnp.float32),
            pltpu.VMEM((LIVE * TILE, DH), jnp.float32),
            pltpu.VMEM((HEADS, LIVE, TILE, DH), bf16),
            pltpu.VMEM((N, ROWS, LOCAL), bf16),
            pltpu.VMEM((8, DH), i32),
            pltpu.VMEM((N, 8, DH), i32),
            pltpu.SMEM((N, 8, DH), i32),
            packets, packets, packets, packets,
            dma((6,)),
            dma((N,)), dma((N,)),
            dma((1,)), dma((1,)),
            dma((2, HOPS + 1, HEADS)), dma((2, HOPS + 1, HEADS)),
            dma((N,)), dma((N,)),
            dma((HEADS, N)), dma((HEADS, N)),
            dma((HEADS, N)), dma((HEADS, N)),
        ],
        name="refresh_attention",
        compiler_params=pltpu.CompilerParams(
            collective_id=0, has_side_effects=True, vmem_limit_bytes=56 * 2**20
        ),
    )(tiles, inverse, q_slots, k_cache, v_cache)


def keep_live(attended, tiles):
    row = lax.broadcasted_iota(jnp.int32, attended.shape, 0)
    tile = jnp.where(row < TILE, tiles[0, 0], tiles[0, 1])
    return jnp.where(tile >= 0, attended, jnp.zeros((), attended.dtype))


def every_slot(q_slots, k_cache, v_cache, tiles):
    width = q_slots.shape[1]
    exchange = functools.partial(lax.all_to_all, axis_name="seq", tiled=True)
    keys = exchange(k_cache, split_axis=1, concat_axis=0)
    values = exchange(v_cache, split_axis=1, concat_axis=0)
    tile = lax.axis_index("seq") * SLOTS + jnp.maximum(tiles[0], 0)
    position = (tile[:, None] * TILE + jnp.arange(TILE, dtype=jnp.int32)).reshape(ROWS, 1, 1).astype(jnp.float32)
    angles = position * 10000.0 ** (-jnp.arange(HALF, dtype=jnp.float32) / HALF)
    cosine, sine = jnp.cos(angles), jnp.sin(angles)
    queries = q_slots.astype(jnp.float32).reshape(ROWS, width // DH, DH)
    a, b = queries[..., :HALF], queries[..., HALF:]
    rotated = jnp.concatenate([a * cosine - b * sine, b * cosine + a * sine], axis=-1)
    rotated = rotated.astype(jnp.bfloat16).reshape(ROWS, width)
    rotated = exchange(rotated, split_axis=1, concat_axis=0)

    def one(index):
        head = lax.rem(index, HEADS)
        rows = lax.dynamic_slice(rotated, (index // HEADS * 512, head * DH), (512, DH))
        head_keys = lax.dynamic_slice_in_dim(keys, head * DH, DH, 1)
        head_values = lax.dynamic_slice_in_dim(values, head * DH, DH, 1)
        logits = jnp.dot(rows, head_keys.T, preferred_element_type=jnp.float32) * DH**-0.5
        weight = jnp.exp(logits - jnp.max(logits, axis=-1, keepdims=True))
        weight = (weight / jnp.sum(weight, axis=-1, keepdims=True)).astype(jnp.bfloat16)
        return jnp.dot(weight, head_values, preferred_element_type=jnp.float32).astype(jnp.bfloat16)

    result = lax.map(one, jnp.arange(N * ROWS // 512 * HEADS))
    result = result.reshape(N * ROWS // 512, HEADS, 512, DH).swapaxes(1, 2).reshape(N * ROWS, LOCAL)
    return keep_live(exchange(result, split_axis=0, concat_axis=1), tiles)


def on_device(q_slots, k_cache, v_cache, tiles):
    attended, misfit = refresh(q_slots, k_cache, v_cache, tiles)
    def other_way():
        rowwise = Layout(major_to_minor=(0, 1))
        given = [with_layout_constraint(array, rowwise) for array in (q_slots, k_cache, v_cache, tiles)]
        return with_layout_constraint(every_slot(*given), rowwise)

    return lax.cond(misfit[0] > 0, other_way, lambda: attended)


def solution(mesh):
    spec = P(("req", "seq"), None)
    return jax.shard_map(
        on_device, mesh=mesh, in_specs=(spec,) * 4, out_specs=spec, check_vma=False
    )
```

```python
import functools
import math

import jax
import jax.numpy as jnp
import numpy as np
from jax import lax
from jax.experimental import pallas as pl
from jax.experimental.layout import Layout, with_layout_constraint
from jax.experimental.pallas import tpu as pltpu
from jax.sharding import PartitionSpec as P

MESH = pl.DeviceIdType.MESH
DH = 128
HALF = DH // 2
TILE = 64
SLOTS = 2
LIVE = 12
HEADS = 2
LOCAL = HEADS * DH
N = 16
CHIPS = N // 2
ROWS = SLOTS * TILE
ROOM = {1: 8, 2: 7, 3: 5, 4: 3, 5: 2, 6: 0, 7: 0}
HOPS = 5
PACE = (10, 1)


def kernel(tiles_in, inv_in, q_ref, k_ref, v_ref, o_ref, flag_ref,
           tiles_ref, inv_ref, q_in, q_out, q_chip, q_live, k_all, v_all, probs, norm, o_sum, o_live, o_send,
           count_out, count_all, counts,
           pack_a, pack_b, land_a, land_b,
           local_sem, count_ssem, count_rsem, twin_ssem, twin_rsem,
           hop_ssem, hop_rsem, k_ssem, k_rsem, v_ssem, v_rsem, o_ssem, o_rsem):
    me = lax.axis_index("seq")
    chip = me // 2
    core = lax.rem(me, 2)

    def at(index, size):
        return pl.ds(pl.multiple_of(index * size, size), size)

    def peer(offset):
        return lax.rem(me + offset, N)

    def remote(source, target, ssem, rsem, **where):
        return pltpu.make_async_remote_copy(
            src_ref=source, dst_ref=target, send_sem=ssem, recv_sem=rsem,
            device_id=where, device_id_type=MESH,
        )

    barrier = pltpu.get_barrier_semaphore()
    for offset in range(1, N):
        pl.semaphore_signal(barrier, inc=1, device_id={"seq": peer(offset)}, device_id_type=MESH)
    load_tiles = pltpu.make_async_copy(tiles_in, tiles_ref, local_sem.at[4])
    load_tiles.start()
    load_inv = pltpu.make_async_copy(inv_in, inv_ref, local_sem.at[5])
    load_inv.start()
    load_q = pltpu.make_async_copy(q_ref, q_in, local_sem.at[0])
    load_q.start()
    own_k = pltpu.make_async_copy(k_ref.at[:, at(me, LOCAL)], k_all.at[at(me, ROWS), :], local_sem.at[1])
    own_k.start()
    own_v = pltpu.make_async_copy(v_ref.at[:, at(me, LOCAL)], v_all.at[at(me, ROWS), :], local_sem.at[2])
    own_v.start()

    load_tiles.wait()
    first_live = (tiles_ref[0, 0] >= 0).astype(jnp.int32)
    second_live = (tiles_ref[0, 1] >= 0).astype(jnp.int32)
    count = jnp.full((8, DH), first_live + second_live, jnp.int32)
    count_out[...] = count
    count_all[me] = count
    row = lax.broadcasted_iota(jnp.int32, (ROWS, DH), 0)
    lane = lax.broadcasted_iota(jnp.int32, (ROWS, DH), 1)
    first = jnp.maximum(tiles_ref[0, 0], 0) * TILE
    second = (jnp.maximum(tiles_ref[0, 1], 0) - 1) * TILE
    position = (me * ROWS + row + jnp.where(row < TILE, first, second)).astype(jnp.float32)
    load_inv.wait()
    angles = position * inv_ref[0:1, :]
    cosine = jnp.cos(angles)
    sine = jnp.sin(angles)
    sine = jnp.where(lane < HALF, -sine, sine)
    load_q.wait()

    def rotate(plane, target, index, carry):
        head = (index // HEADS * 2 + plane) * HEADS + lax.rem(index, HEADS)
        value = q_in[:, at(head, DH)].astype(jnp.float32)
        swapped = pltpu.roll(value, HALF, axis=1)
        turned = (value * cosine + swapped * sine).astype(jnp.bfloat16)
        for slot in range(SLOTS):
            target[slot, :, at(index, DH)] = turned[slot * TILE:(slot + 1) * TILE, :]
        return carry

    mine = q_chip.at[pl.ds(core * SLOTS, SLOTS)]
    lax.fori_loop(0, CHIPS * HEADS, functools.partial(rotate, 1 - core, q_out), 0)
    pl.semaphore_wait(barrier, N - 1)

    def send_count(offset):
        return remote(count_out, count_all.at[me], count_ssem.at[offset], count_rsem.at[offset], seq=peer(offset))

    def send_k(offset):
        to = peer(offset)
        return remote(k_ref.at[:, at(to, LOCAL)], k_all.at[at(me, ROWS), :],
                      k_ssem.at[offset], k_rsem.at[offset], seq=to)

    def send_v(head, offset):
        to = peer(offset)
        return remote(v_ref.at[:, at(to * HEADS + head, DH)], v_all.at[at(me, ROWS), pl.ds(head * DH, DH)],
                      v_ssem.at[head, offset], v_rsem.at[head, offset], seq=to)

    def send_o(head, offset):
        to = peer(offset)
        return remote(o_send.at[offset, :, pl.ds(head * DH, DH)], o_ref.at[:, at(me * HEADS + head, DH)],
                      o_ssem.at[head, offset], o_rsem.at[head, offset], seq=to)

    order = []
    for step in range(1, N // 2 + 1):
        order += [step] if step == N // 2 else [step, N - step]
    bulk = [send_k(offset) for offset in order]
    bulk += [send_v(head, offset) for head in range(HEADS) for offset in order]
    started = 0

    def start_bulk(amount):
        nonlocal started
        for copy in bulk[started:started + amount]:
            copy.start()
        started += amount

    for offset in order:
        send_count(offset).start()
    twin = remote(q_out, mine, twin_ssem.at[0], twin_rsem.at[0], seq=chip * 2 + 1 - core)
    twin.start()
    start_bulk(PACE[0])

    lax.fori_loop(0, CHIPS * HEADS, functools.partial(rotate, core, mine), 0)

    for offset in order:
        send_count(offset).wait_recv()
    to_scalar = pltpu.make_async_copy(count_all, counts, local_sem.at[3])
    to_scalar.start()
    to_scalar.wait()

    def count_of(offset, which):
        return counts[lax.rem(chip + offset, CHIPS) * 2 + which, 0, 0]

    first_core = [count_of(offset, 0) for offset in range(CHIPS)]
    there = [first_core[offset] + count_of(offset, 1) for offset in range(CHIPS)]
    below, above, by_a, by_b, total = [], [], [], [], []
    misfit = jnp.int32(0)
    for to in range(CHIPS):
        near_a, near_b = [jnp.int32(0)], [jnp.int32(0)]
        for away in range(1, CHIPS):
            near_a.append(near_a[-1] + there[(to - away) % CHIPS])
            near_b.append(near_b[-1] + there[(to + away) % CHIPS])
        whole = near_a[-1]
        fit_a = fit_b = whole
        for away in range(1, CHIPS):
            fit_a = jnp.minimum(fit_a, near_a[away - 1] + ROOM[away])
            fit_b = jnp.minimum(fit_b, near_b[away - 1] + ROOM[away])
        misfit = jnp.maximum(misfit, whole - fit_a - fit_b)
        below.append(near_a)
        above.append(near_b)
        by_a.append(fit_a)
        by_b.append(whole - fit_a)
        total.append(whole)

    flag_ref[0] = misfit

    def tile_at(rank):
        index = jnp.where(rank < first_core[0], rank, rank + SLOTS - first_core[0])
        return jnp.clip(index, 0, 2 * SLOTS - 1)

    def hop(side, hops, head):
        pack, land, to = ((pack_a, land_a, 2), (pack_b, land_b, N - 2))[side]
        slots = pl.ds(hops * 8, ROOM[hops])
        return remote(pack.at[head, slots], land.at[head, slots], hop_ssem.at[side, hops, head],
                      hop_rsem.at[side, hops, head], seq=peer(to))

    twin.wait_recv()
    for hops in range(HOPS, 0, -1):
        to_a, to_b = hops, CHIPS - hops
        for head in range(HEADS):
            if hops < HOPS:
                hop(0, hops + 1, head).wait_recv()
                hop(1, hops + 1, head).wait_recv()
            column_a = at(lax.rem(chip + to_a, CHIPS) * HEADS + head, DH)
            column_b = at(lax.rem(chip + to_b, CHIPS) * HEADS + head, DH)
            for slot in range(ROOM[hops]):
                rank = by_a[to_a] - 1 - slot - below[to_a][hops - 1]
                value = q_chip[tile_at(rank), :, column_a]
                if slot < ROOM[hops + 1]:
                    is_mine = jnp.logical_and(rank >= 0, rank < there[0])
                    value = jnp.where(is_mine, value, land_a[head, (hops + 1) * 8 + slot])
                pack_a[head, hops * 8 + slot] = value
                rank = by_b[to_b] - 1 - slot - above[to_b][hops - 1]
                value = q_chip[tile_at(there[0] - 1 - rank), :, column_b]
                if slot < ROOM[hops + 1]:
                    is_mine = jnp.logical_and(rank >= 0, rank < there[0])
                    value = jnp.where(is_mine, value, land_b[head, (hops + 1) * 8 + slot])
                pack_b[head, hops * 8 + slot] = value
            hop(0, hops, head).start()
            hop(1, hops, head).start()
            start_bulk(PACE[1])
    start_bulk(len(bulk) - started)

    for head in range(HEADS):
        hop(0, 1, head).wait_recv()
        hop(1, 1, head).wait_recv()
    for head in range(HEADS):
        column = at(chip * HEADS + head, DH)
        columns = pl.ds(head * DH, DH)
        for slot in range(LIVE):
            value = q_chip[tile_at(slot - total[0]), :, column]
            other = land_b[head, 8 + jnp.clip(slot - by_a[0], 0, 7)]
            value = jnp.where(slot < total[0], other, value)
            if slot < ROOM[1]:
                value = jnp.where(slot < by_a[0], land_a[head, 8 + slot], value)
            q_live[slot * TILE:(slot + 1) * TILE, columns] = value

    own_k.wait()
    for offset in order:
        send_k(offset).wait_recv()

    factor = math.log2(math.e) / math.sqrt(DH)
    block = 2 * TILE

    def score(index, carry):
        for head in range(HEADS):
            columns = pl.ds(head * DH, DH)
            logits = lax.dot_general(
                q_live[at(index, block), columns], k_all[:, columns],
                (((1,), (1,)), ((), ())), preferred_element_type=jnp.float32,
            )
            largest = jnp.max(logits, axis=1, keepdims=True)
            weight = jnp.exp2((logits - largest) * factor)
            norm[at(index, block), columns] = jnp.broadcast_to(
                1.0 / jnp.sum(weight, axis=1, keepdims=True), (block, DH)
            )
            probs[head, at(index, block), :] = weight.astype(jnp.bfloat16)
        return carry

    lax.fori_loop(0, LIVE * TILE // block, score, 0)

    places = {}
    for offset in order + [0]:
        home = peer(offset)
        back = CHIPS - lax.rem(home // 2 - chip + CHIPS, CHIPS)
        before = jnp.int32(0)
        for step in range(1, CHIPS):
            before = jnp.where(back == step, below[0][step - 1], before)
        rank = jnp.where(lax.rem(home, 2) == 0, 0, counts[home // 2 * 2, 0, 0])
        for slot in range(SLOTS):
            index = before + rank + slot
            index = jnp.where(index < by_a[0], by_a[0] - 1 - index, index)
            index = jnp.where(back == CHIPS, total[0] + rank + slot, index)
            places[offset, slot] = jnp.clip(index, 0, LIVE - 1)

    own_v.wait()
    for head in range(HEADS):
        columns = pl.ds(head * DH, DH)
        for step, away in enumerate((0, 1, 7, 2, 6, 3, 5, 4)):
            if away == 0:
                send_v(head, lax.rem(N + 2 * core - 1, N)).wait_recv()
            else:
                for which in range(2):
                    send_v(head, 2 * away + core - which).wait_recv()
            rows = at(lax.rem(chip - away + CHIPS, CHIPS), 2 * ROWS)
            product = jnp.dot(probs[head, :, rows], v_all[rows, columns], preferred_element_type=jnp.float32)
            if step == 0:
                o_sum[...] = product
            elif step < CHIPS - 1:
                o_sum[...] += product
            else:
                product = ((o_sum[...] + product) * norm[:, columns]).astype(jnp.bfloat16)
                for slot in range(LIVE):
                    o_live[head, slot] = product[slot * TILE:(slot + 1) * TILE, :]
        for offset in order + [0]:
            for slot in range(SLOTS):
                o_send[offset, slot * TILE:(slot + 1) * TILE, columns] = o_live[head, places[offset, slot]]
            if offset > 0:
                send_o(head, offset).start()
    o_ref[:, at(me, LOCAL)] = o_send[0]

    for offset in order:
        send_count(offset).wait_send()
    twin.wait_send()
    for hops in range(1, HOPS + 1):
        for head in range(HEADS):
            hop(0, hops, head).wait_send()
            hop(1, hops, head).wait_send()
    for copy in bulk:
        copy.wait_send()
    for head in range(HEADS):
        for offset in order:
            send_o(head, offset).wait()
    for slot in range(SLOTS):
        rows = pl.ds(slot * TILE, TILE)
        o_ref[rows, :] = jnp.where(tiles_ref[0, slot] >= 0, o_ref[rows, :], jnp.zeros((), jnp.bfloat16))


def refresh(q_slots, k_cache, v_cache, tiles):
    width = q_slots.shape[1]
    inverse = 10000.0 ** (-np.arange(HALF) / HALF)
    inverse = jnp.asarray(np.broadcast_to(np.tile(inverse, 2)[None, :], (8, DH)), jnp.float32)
    dma = pltpu.SemaphoreType.DMA
    bf16, i32 = jnp.bfloat16, jnp.int32
    packets = pltpu.VMEM((HEADS, (HOPS + 1) * 8, TILE, DH), bf16)
    return pl.pallas_call(
        kernel,
        out_shape=(
            jax.ShapeDtypeStruct((ROWS, width), bf16),
            jax.ShapeDtypeStruct((1,), i32),
        ),
        in_specs=[
            pl.BlockSpec(memory_space=pl.ANY),
            pl.BlockSpec(memory_space=pl.ANY),
            pl.BlockSpec(memory_space=pl.ANY),
            pl.BlockSpec(memory_space=pl.ANY),
            pl.BlockSpec(memory_space=pl.ANY),
        ],
        out_specs=(pl.BlockSpec(memory_space=pltpu.VMEM), pl.BlockSpec(memory_space=pltpu.SMEM)),
        scratch_shapes=[
            pltpu.SMEM((1, SLOTS), i32),
            pltpu.VMEM((8, DH), jnp.float32),
            pltpu.VMEM((ROWS, width), bf16),
            pltpu.VMEM((SLOTS, TILE, width // 2), bf16),
            pltpu.VMEM((2 * SLOTS, TILE, width // 2), bf16),
            pltpu.VMEM((LIVE * TILE, LOCAL), bf16),
            pltpu.VMEM((N * ROWS, LOCAL), bf16),
            pltpu.VMEM((N * ROWS, LOCAL), bf16),
            pltpu.VMEM((HEADS, LIVE * TILE, N * ROWS), bf16),
            pltpu.VMEM((LIVE * TILE, LOCAL), jnp.float32),
            pltpu.VMEM((LIVE * TILE, DH), jnp.float32),
            pltpu.VMEM((HEADS, LIVE, TILE, DH), bf16),
            pltpu.VMEM((N, ROWS, LOCAL), bf16),
            pltpu.VMEM((8, DH), i32),
            pltpu.VMEM((N, 8, DH), i32),
            pltpu.SMEM((N, 8, DH), i32),
            packets, packets, packets, packets,
            dma((6,)),
            dma((N,)), dma((N,)),
            dma((1,)), dma((1,)),
            dma((2, HOPS + 1, HEADS)), dma((2, HOPS + 1, HEADS)),
            dma((N,)), dma((N,)),
            dma((HEADS, N)), dma((HEADS, N)),
            dma((HEADS, N)), dma((HEADS, N)),
        ],
        name="refresh_attention",
        compiler_params=pltpu.CompilerParams(
            collective_id=0, has_side_effects=True, vmem_limit_bytes=56 * 2**20
        ),
    )(tiles, inverse, q_slots, k_cache, v_cache)


def keep_live(attended, tiles):
    row = lax.broadcasted_iota(jnp.int32, attended.shape, 0)
    tile = jnp.where(row < TILE, tiles[0, 0], tiles[0, 1])
    return jnp.where(tile >= 0, attended, jnp.zeros((), attended.dtype))


def every_slot(q_slots, k_cache, v_cache, tiles):
    width = q_slots.shape[1]
    exchange = functools.partial(lax.all_to_all, axis_name="seq", tiled=True)
    keys = exchange(k_cache, split_axis=1, concat_axis=0)
    values = exchange(v_cache, split_axis=1, concat_axis=0)
    tile = lax.axis_index("seq") * SLOTS + jnp.maximum(tiles[0], 0)
    position = (tile[:, None] * TILE + jnp.arange(TILE, dtype=jnp.int32)).reshape(ROWS, 1, 1).astype(jnp.float32)
    angles = position * 10000.0 ** (-jnp.arange(HALF, dtype=jnp.float32) / HALF)
    cosine, sine = jnp.cos(angles), jnp.sin(angles)
    queries = q_slots.astype(jnp.float32).reshape(ROWS, width // DH, DH)
    a, b = queries[..., :HALF], queries[..., HALF:]
    rotated = jnp.concatenate([a * cosine - b * sine, b * cosine + a * sine], axis=-1)
    rotated = rotated.astype(jnp.bfloat16).reshape(ROWS, width)
    rotated = exchange(rotated, split_axis=1, concat_axis=0)

    def one(index):
        head = lax.rem(index, HEADS)
        rows = lax.dynamic_slice(rotated, (index // HEADS * 512, head * DH), (512, DH))
        head_keys = lax.dynamic_slice_in_dim(keys, head * DH, DH, 1)
        head_values = lax.dynamic_slice_in_dim(values, head * DH, DH, 1)
        logits = jnp.dot(rows, head_keys.T, preferred_element_type=jnp.float32) * DH**-0.5
        weight = jnp.exp(logits - jnp.max(logits, axis=-1, keepdims=True))
        weight = (weight / jnp.sum(weight, axis=-1, keepdims=True)).astype(jnp.bfloat16)
        return jnp.dot(weight, head_values, preferred_element_type=jnp.float32).astype(jnp.bfloat16)

    result = lax.map(one, jnp.arange(N * ROWS // 512 * HEADS))
    result = result.reshape(N * ROWS // 512, HEADS, 512, DH).swapaxes(1, 2).reshape(N * ROWS, LOCAL)
    return keep_live(exchange(result, split_axis=0, concat_axis=1), tiles)


def on_device(q_slots, k_cache, v_cache, tiles):
    attended, misfit = refresh(q_slots, k_cache, v_cache, tiles)
    def other_way():
        rowwise = Layout(major_to_minor=(0, 1))
        given = [with_layout_constraint(array, rowwise) for array in (q_slots, k_cache, v_cache, tiles)]
        return with_layout_constraint(every_slot(*given), rowwise)

    return lax.cond(misfit[0] > 0, other_way, lambda: attended)


def solution(mesh):
    spec = P(("req", "seq"), None)
    return jax.shard_map(
        on_device, mesh=mesh, in_specs=(spec,) * 4, out_specs=spec, check_vma=False
    )
```

```python
import functools
import math

import jax
import jax.numpy as jnp
import numpy as np
from jax import lax
from jax.experimental import pallas as pl
from jax.experimental.layout import Layout, with_layout_constraint
from jax.experimental.pallas import tpu as pltpu
from jax.sharding import PartitionSpec as P

MESH = pl.DeviceIdType.MESH
DH = 128
HALF = DH // 2
TILE = 64
SLOTS = 2
LIVE = 12
HEADS = 2
LOCAL = HEADS * DH
N = 16
CHIPS = N // 2
ROWS = SLOTS * TILE
ROOM = {1: 8, 2: 7, 3: 5, 4: 3, 5: 2, 6: 0, 7: 0}
HOPS = 5
PACE = (8, 1)


def kernel(tiles_in, inv_in, q_ref, k_ref, v_ref, o_ref, flag_ref,
           tiles_ref, inv_ref, q_in, q_out, q_chip, q_live, k_all, v_all, probs, norm, o_sum, o_live, o_send,
           count_out, count_all, counts,
           pack_a, pack_b, land_a, land_b,
           local_sem, count_ssem, count_rsem, twin_ssem, twin_rsem,
           hop_ssem, hop_rsem, k_ssem, k_rsem, v_ssem, v_rsem, o_ssem, o_rsem):
    me = lax.axis_index("seq")
    chip = me // 2
    core = lax.rem(me, 2)

    def at(index, size):
        return pl.ds(pl.multiple_of(index * size, size), size)

    def peer(offset):
        return lax.rem(me + offset, N)

    def remote(source, target, ssem, rsem, **where):
        return pltpu.make_async_remote_copy(
            src_ref=source, dst_ref=target, send_sem=ssem, recv_sem=rsem,
            device_id=where, device_id_type=MESH,
        )

    barrier = pltpu.get_barrier_semaphore()
    for offset in range(1, N):
        pl.semaphore_signal(barrier, inc=1, device_id={"seq": peer(offset)}, device_id_type=MESH)
    load_tiles = pltpu.make_async_copy(tiles_in, tiles_ref, local_sem.at[4])
    load_tiles.start()
    load_inv = pltpu.make_async_copy(inv_in, inv_ref, local_sem.at[5])
    load_inv.start()
    load_q = pltpu.make_async_copy(q_ref, q_in, local_sem.at[0])
    load_q.start()
    own_k = pltpu.make_async_copy(k_ref.at[:, at(me, LOCAL)], k_all.at[at(me, ROWS), :], local_sem.at[1])
    own_k.start()
    own_v = pltpu.make_async_copy(v_ref.at[:, at(me, LOCAL)], v_all.at[at(me, ROWS), :], local_sem.at[2])
    own_v.start()

    load_tiles.wait()
    first_live = (tiles_ref[0, 0] >= 0).astype(jnp.int32)
    second_live = (tiles_ref[0, 1] >= 0).astype(jnp.int32)
    count = jnp.full((8, DH), first_live + second_live, jnp.int32)
    count_out[...] = count
    count_all[me] = count
    row = lax.broadcasted_iota(jnp.int32, (ROWS, DH), 0)
    lane = lax.broadcasted_iota(jnp.int32, (ROWS, DH), 1)
    first = jnp.maximum(tiles_ref[0, 0], 0) * TILE
    second = (jnp.maximum(tiles_ref[0, 1], 0) - 1) * TILE
    position = (me * ROWS + row + jnp.where(row < TILE, first, second)).astype(jnp.float32)
    load_inv.wait()
    angles = position * inv_ref[0:1, :]
    cosine = jnp.cos(angles)
    sine = jnp.sin(angles)
    sine = jnp.where(lane < HALF, -sine, sine)
    load_q.wait()

    def rotate(plane, target, index, carry):
        head = (index // HEADS * 2 + plane) * HEADS + lax.rem(index, HEADS)
        value = q_in[:, at(head, DH)].astype(jnp.float32)
        swapped = pltpu.roll(value, HALF, axis=1)
        turned = (value * cosine + swapped * sine).astype(jnp.bfloat16)
        for slot in range(SLOTS):
            target[slot, :, at(index, DH)] = turned[slot * TILE:(slot + 1) * TILE, :]
        return carry

    mine = q_chip.at[pl.ds(core * SLOTS, SLOTS)]
    lax.fori_loop(0, CHIPS * HEADS, functools.partial(rotate, 1 - core, q_out), 0)
    pl.semaphore_wait(barrier, N - 1)

    def send_count(offset):
        return remote(count_out, count_all.at[me], count_ssem.at[offset], count_rsem.at[offset], seq=peer(offset))

    def send_k(offset):
        to = peer(offset)
        return remote(k_ref.at[:, at(to, LOCAL)], k_all.at[at(me, ROWS), :],
                      k_ssem.at[offset], k_rsem.at[offset], seq=to)

    def send_v(head, offset):
        to = peer(offset)
        return remote(v_ref.at[:, at(to * HEADS + head, DH)], v_all.at[at(me, ROWS), pl.ds(head * DH, DH)],
                      v_ssem.at[head, offset], v_rsem.at[head, offset], seq=to)

    def send_o(head, offset):
        to = peer(offset)
        return remote(o_send.at[offset, :, pl.ds(head * DH, DH)], o_ref.at[:, at(me * HEADS + head, DH)],
                      o_ssem.at[head, offset], o_rsem.at[head, offset], seq=to)

    order = []
    for step in range(1, N // 2 + 1):
        order += [step] if step == N // 2 else [step, N - step]
    bulk = [send_k(offset) for offset in order]
    bulk += [send_v(head, offset) for head in range(HEADS) for offset in order]
    started = 0

    def start_bulk(amount):
        nonlocal started
        for copy in bulk[started:started + amount]:
            copy.start()
        started += amount

    for offset in order:
        send_count(offset).start()
    twin = remote(q_out, mine, twin_ssem.at[0], twin_rsem.at[0], seq=chip * 2 + 1 - core)
    twin.start()
    start_bulk(PACE[0])

    lax.fori_loop(0, CHIPS * HEADS, functools.partial(rotate, core, mine), 0)

    for offset in order:
        send_count(offset).wait_recv()
    to_scalar = pltpu.make_async_copy(count_all, counts, local_sem.at[3])
    to_scalar.start()
    to_scalar.wait()

    def count_of(offset, which):
        return counts[lax.rem(chip + offset, CHIPS) * 2 + which, 0, 0]

    first_core = [count_of(offset, 0) for offset in range(CHIPS)]
    there = [first_core[offset] + count_of(offset, 1) for offset in range(CHIPS)]
    below, above, by_a, by_b, total = [], [], [], [], []
    misfit = jnp.int32(0)
    for to in range(CHIPS):
        near_a, near_b = [jnp.int32(0)], [jnp.int32(0)]
        for away in range(1, CHIPS):
            near_a.append(near_a[-1] + there[(to - away) % CHIPS])
            near_b.append(near_b[-1] + there[(to + away) % CHIPS])
        whole = near_a[-1]
        fit_a = fit_b = whole
        for away in range(1, CHIPS):
            fit_a = jnp.minimum(fit_a, near_a[away - 1] + ROOM[away])
            fit_b = jnp.minimum(fit_b, near_b[away - 1] + ROOM[away])
        misfit = jnp.maximum(misfit, whole - fit_a - fit_b)
        below.append(near_a)
        above.append(near_b)
        by_a.append(fit_a)
        by_b.append(whole - fit_a)
        total.append(whole)

    flag_ref[0] = misfit

    def tile_at(rank):
        index = jnp.where(rank < first_core[0], rank, rank + SLOTS - first_core[0])
        return jnp.clip(index, 0, 2 * SLOTS - 1)

    def hop(side, hops, head):
        pack, land, to = ((pack_a, land_a, 2), (pack_b, land_b, N - 2))[side]
        slots = pl.ds(hops * 8, ROOM[hops])
        return remote(pack.at[head, slots], land.at[head, slots], hop_ssem.at[side, hops, head],
                      hop_rsem.at[side, hops, head], seq=peer(to))

    twin.wait_recv()
    for hops in range(HOPS, 0, -1):
        to_a, to_b = hops, CHIPS - hops
        for head in range(HEADS):
            if hops < HOPS:
                hop(0, hops + 1, head).wait_recv()
                hop(1, hops + 1, head).wait_recv()
            column_a = at(lax.rem(chip + to_a, CHIPS) * HEADS + head, DH)
            column_b = at(lax.rem(chip + to_b, CHIPS) * HEADS + head, DH)
            for slot in range(ROOM[hops]):
                rank = by_a[to_a] - 1 - slot - below[to_a][hops - 1]
                value = q_chip[tile_at(rank), :, column_a]
                if slot < ROOM[hops + 1]:
                    is_mine = jnp.logical_and(rank >= 0, rank < there[0])
                    value = jnp.where(is_mine, value, land_a[head, (hops + 1) * 8 + slot])
                pack_a[head, hops * 8 + slot] = value
                rank = by_b[to_b] - 1 - slot - above[to_b][hops - 1]
                value = q_chip[tile_at(there[0] - 1 - rank), :, column_b]
                if slot < ROOM[hops + 1]:
                    is_mine = jnp.logical_and(rank >= 0, rank < there[0])
                    value = jnp.where(is_mine, value, land_b[head, (hops + 1) * 8 + slot])
                pack_b[head, hops * 8 + slot] = value
            hop(0, hops, head).start()
            hop(1, hops, head).start()
            start_bulk(PACE[1])
    start_bulk(len(bulk) - started)

    for head in range(HEADS):
        hop(0, 1, head).wait_recv()
        hop(1, 1, head).wait_recv()
    for head in range(HEADS):
        column = at(chip * HEADS + head, DH)
        columns = pl.ds(head * DH, DH)
        for slot in range(LIVE):
            value = q_chip[tile_at(slot - total[0]), :, column]
            other = land_b[head, 8 + jnp.clip(slot - by_a[0], 0, 7)]
            value = jnp.where(slot < total[0], other, value)
            if slot < ROOM[1]:
                value = jnp.where(slot < by_a[0], land_a[head, 8 + slot], value)
            q_live[slot * TILE:(slot + 1) * TILE, columns] = value

    own_k.wait()
    for offset in order:
        send_k(offset).wait_recv()

    factor = math.log2(math.e) / math.sqrt(DH)
    block = 2 * TILE

    def score(index, carry):
        for head in range(HEADS):
            columns = pl.ds(head * DH, DH)
            logits = lax.dot_general(
                q_live[at(index, block), columns], k_all[:, columns],
                (((1,), (1,)), ((), ())), preferred_element_type=jnp.float32,
            )
            largest = jnp.max(logits, axis=1, keepdims=True)
            weight = jnp.exp2((logits - largest) * factor)
            norm[at(index, block), columns] = jnp.broadcast_to(
                1.0 / jnp.sum(weight, axis=1, keepdims=True), (block, DH)
            )
            probs[head, at(index, block), :] = weight.astype(jnp.bfloat16)
        return carry

    lax.fori_loop(0, LIVE * TILE // block, score, 0)

    places, alive = {}, {}
    for offset in order + [0]:
        home = peer(offset)
        alive[offset] = counts[home, 0, 0]
        back = CHIPS - lax.rem(home // 2 - chip + CHIPS, CHIPS)
        before = jnp.int32(0)
        for step in range(1, CHIPS):
            before = jnp.where(back == step, below[0][step - 1], before)
        rank = jnp.where(lax.rem(home, 2) == 0, 0, counts[home // 2 * 2, 0, 0])
        for slot in range(SLOTS):
            index = before + rank + slot
            index = jnp.where(index < by_a[0], by_a[0] - 1 - index, index)
            index = jnp.where(back == CHIPS, total[0] + rank + slot, index)
            places[offset, slot] = jnp.clip(index, 0, LIVE - 1)

    own_v.wait()
    for head in range(HEADS):
        columns = pl.ds(head * DH, DH)
        for step, away in enumerate((0, 1, 7, 2, 6, 3, 5, 4)):
            if away == 0:
                send_v(head, lax.rem(N + 2 * core - 1, N)).wait_recv()
            else:
                for which in range(2):
                    send_v(head, 2 * away + core - which).wait_recv()
            rows = at(lax.rem(chip - away + CHIPS, CHIPS), 2 * ROWS)
            product = jnp.dot(probs[head, :, rows], v_all[rows, columns], preferred_element_type=jnp.float32)
            if step == 0:
                o_sum[...] = product
            elif step < CHIPS - 1:
                o_sum[...] += product
            else:
                product = ((o_sum[...] + product) * norm[:, columns]).astype(jnp.bfloat16)
                for slot in range(LIVE):
                    o_live[head, slot] = product[slot * TILE:(slot + 1) * TILE, :]
        for offset in order + [0]:
            for slot in range(SLOTS):
                value = o_live[head, places[offset, slot]]
                value = jnp.where(slot < alive[offset], value, jnp.zeros((), jnp.bfloat16))
                o_send[offset, slot * TILE:(slot + 1) * TILE, columns] = value
            if offset > 0:
                send_o(head, offset).start()
    o_ref[:, at(me, LOCAL)] = o_send[0]

    for offset in order:
        send_count(offset).wait_send()
    twin.wait_send()
    for hops in range(1, HOPS + 1):
        for head in range(HEADS):
            hop(0, hops, head).wait_send()
            hop(1, hops, head).wait_send()
    for copy in bulk:
        copy.wait_send()
    for head in range(HEADS):
        for offset in order:
            send_o(head, offset).wait()


def refresh(q_slots, k_cache, v_cache, tiles):
    width = q_slots.shape[1]
    inverse = 10000.0 ** (-np.arange(HALF) / HALF)
    inverse = jnp.asarray(np.broadcast_to(np.tile(inverse, 2)[None, :], (8, DH)), jnp.float32)
    dma = pltpu.SemaphoreType.DMA
    bf16, i32 = jnp.bfloat16, jnp.int32
    packets = pltpu.VMEM((HEADS, (HOPS + 1) * 8, TILE, DH), bf16)
    return pl.pallas_call(
        kernel,
        out_shape=(
            jax.ShapeDtypeStruct((ROWS, width), bf16),
            jax.ShapeDtypeStruct((1,), i32),
        ),
        in_specs=[
            pl.BlockSpec(memory_space=pl.ANY),
            pl.BlockSpec(memory_space=pl.ANY),
            pl.BlockSpec(memory_space=pl.ANY),
            pl.BlockSpec(memory_space=pl.ANY),
            pl.BlockSpec(memory_space=pl.ANY),
        ],
        out_specs=(pl.BlockSpec(memory_space=pltpu.VMEM), pl.BlockSpec(memory_space=pltpu.SMEM)),
        scratch_shapes=[
            pltpu.SMEM((1, SLOTS), i32),
            pltpu.VMEM((8, DH), jnp.float32),
            pltpu.VMEM((ROWS, width), bf16),
            pltpu.VMEM((SLOTS, TILE, width // 2), bf16),
            pltpu.VMEM((2 * SLOTS, TILE, width // 2), bf16),
            pltpu.VMEM((LIVE * TILE, LOCAL), bf16),
            pltpu.VMEM((N * ROWS, LOCAL), bf16),
            pltpu.VMEM((N * ROWS, LOCAL), bf16),
            pltpu.VMEM((HEADS, LIVE * TILE, N * ROWS), bf16),
            pltpu.VMEM((LIVE * TILE, LOCAL), jnp.float32),
            pltpu.VMEM((LIVE * TILE, DH), jnp.float32),
            pltpu.VMEM((HEADS, LIVE, TILE, DH), bf16),
            pltpu.VMEM((N, ROWS, LOCAL), bf16),
            pltpu.VMEM((8, DH), i32),
            pltpu.VMEM((N, 8, DH), i32),
            pltpu.SMEM((N, 8, DH), i32),
            packets, packets, packets, packets,
            dma((6,)),
            dma((N,)), dma((N,)),
            dma((1,)), dma((1,)),
            dma((2, HOPS + 1, HEADS)), dma((2, HOPS + 1, HEADS)),
            dma((N,)), dma((N,)),
            dma((HEADS, N)), dma((HEADS, N)),
            dma((HEADS, N)), dma((HEADS, N)),
        ],
        name="refresh_attention",
        compiler_params=pltpu.CompilerParams(
            collective_id=0, has_side_effects=True, vmem_limit_bytes=56 * 2**20
        ),
    )(tiles, inverse, q_slots, k_cache, v_cache)


def keep_live(attended, tiles):
    row = lax.broadcasted_iota(jnp.int32, attended.shape, 0)
    tile = jnp.where(row < TILE, tiles[0, 0], tiles[0, 1])
    return jnp.where(tile >= 0, attended, jnp.zeros((), attended.dtype))


def every_slot(q_slots, k_cache, v_cache, tiles):
    width = q_slots.shape[1]
    exchange = functools.partial(lax.all_to_all, axis_name="seq", tiled=True)
    keys = exchange(k_cache, split_axis=1, concat_axis=0)
    values = exchange(v_cache, split_axis=1, concat_axis=0)
    tile = lax.axis_index("seq") * SLOTS + jnp.maximum(tiles[0], 0)
    position = (tile[:, None] * TILE + jnp.arange(TILE, dtype=jnp.int32)).reshape(ROWS, 1, 1).astype(jnp.float32)
    angles = position * 10000.0 ** (-jnp.arange(HALF, dtype=jnp.float32) / HALF)
    cosine, sine = jnp.cos(angles), jnp.sin(angles)
    queries = q_slots.astype(jnp.float32).reshape(ROWS, width // DH, DH)
    a, b = queries[..., :HALF], queries[..., HALF:]
    rotated = jnp.concatenate([a * cosine - b * sine, b * cosine + a * sine], axis=-1)
    rotated = rotated.astype(jnp.bfloat16).reshape(ROWS, width)
    rotated = exchange(rotated, split_axis=1, concat_axis=0)

    def one(index):
        head = lax.rem(index, HEADS)
        rows = lax.dynamic_slice(rotated, (index // HEADS * 512, head * DH), (512, DH))
        head_keys = lax.dynamic_slice_in_dim(keys, head * DH, DH, 1)
        head_values = lax.dynamic_slice_in_dim(values, head * DH, DH, 1)
        logits = jnp.dot(rows, head_keys.T, preferred_element_type=jnp.float32) * DH**-0.5
        weight = jnp.exp(logits - jnp.max(logits, axis=-1, keepdims=True))
        weight = (weight / jnp.sum(weight, axis=-1, keepdims=True)).astype(jnp.bfloat16)
        return jnp.dot(weight, head_values, preferred_element_type=jnp.float32).astype(jnp.bfloat16)

    result = lax.map(one, jnp.arange(N * ROWS // 512 * HEADS))
    result = result.reshape(N * ROWS // 512, HEADS, 512, DH).swapaxes(1, 2).reshape(N * ROWS, LOCAL)
    return keep_live(exchange(result, split_axis=0, concat_axis=1), tiles)


def on_device(q_slots, k_cache, v_cache, tiles):
    attended, misfit = refresh(q_slots, k_cache, v_cache, tiles)
    def other_way():
        rowwise = Layout(major_to_minor=(0, 1))
        given = [with_layout_constraint(array, rowwise) for array in (q_slots, k_cache, v_cache, tiles)]
        return with_layout_constraint(every_slot(*given), rowwise)

    return lax.cond(misfit[0] > 0, other_way, lambda: attended)


def solution(mesh):
    spec = P(("req", "seq"), None)
    return jax.shard_map(
        on_device, mesh=mesh, in_specs=(spec,) * 4, out_specs=spec, check_vma=False
    )
```
